256 devices in a mesh: gx: 16 (over x, z_hi, core), gy: 4 (over y), gz: 4 (over z_lo).
Axes of the slice: x: 4, y: 4, z: 8 (z_hi: 2, z_lo: 4; z = z_hi * 4 + z_lo), core: 2. Of those that a mesh axis runs over, the one named last changes fastest.
Arguments:
- populations: float32 [19, 128, 32, 512], P(None, 'gx', 'gy', 'gz'), may hold values from 0 to 1, as said below
- adjoint_seed: float32 [19, 128, 32, 512], P(None, 'gx', 'gy', 'gz'), may hold values from -6 to 6
- wall_slip: float32 [128, 32, 512], P('gx', 'gy', 'gz'), may hold values from 0.1 to 0.9
- permeability: float32 [128, 32, 512], P('gx', 'gy', 'gz'), may hold values from 0.2 to 0.95
- cell_kinds: int32 [128, 32, 512], P('gx', 'gy', 'gz'), may hold values from 0 to 2
Outputs:
- grad_populations: float32 [19, 128, 32, 512], P(None, 'gx', 'gy', 'gz')
- grad_slip: float32 [128, 32, 512], P('gx', 'gy', 'gz')
- grad_permeability: float32 [128, 32, 512], P('gx', 'gy', 'gz')
The draws below stay inside these ranges and needn't reach their ends.
Inputs may be any that keep to these rules, and one draw needn't show every extreme that they name: `populations`: each population is its lattice weight times a factor between 0.25 and 1.75.
All inputs are finite; a program needn't handle non-finite values.
Results may differ from the reference program's by a relative error of at most 0.0003.
Values sent between devices are 32-bit elements; how exact they have to be, the bound alone decides.
A program may use at most 64 MiB of HBM per device.

```python
import jax
import jax.numpy as jnp
import numpy as np
from jax import lax

Q = 19
NX = 128
NY = 32
NZ = 512


WEIGHT = np.array([1.0 / 3.0] + [1.0 / 18.0] * 6 + [1.0 / 36.0] * 12)


def draw_populations(key, part):
    key = jax.random.fold_in(key, 7)
    weights = jnp.asarray(WEIGHT, jnp.float32).reshape(19, 1, 1, 1)
    noise = jnp.clip(0.25 * jax.random.normal(key, (Q, NX, NY, NZ), jnp.float32), -0.75, 0.75)
    return weights * (1.0 + noise)


def touch_ends(result, stream_key, smallest, high):
    longest = result.shape.index(max(result.shape))
    spots = []
    for shift in (0, 1):
        where = [jax.random.randint(jax.random.fold_in(stream_key, axis), (), 0, length) for axis, length in enumerate(result.shape)]
        where[longest] = (where[longest] + shift) % result.shape[longest]
        spots.append(tuple(where))
    return result.at[spots[0]].set(smallest).at[spots[1]].set(high)


def steps_of(key, shape, cuts, smallest, high):
    factor_of = 1.0
    for position, blocks in cuts:
        heights = jax.random.uniform(jax.random.fold_in(jax.random.fold_in(key, 6), position), (blocks,), jnp.float32, smallest / len(cuts), high / len(cuts))
        factor_of = factor_of * jnp.repeat(jnp.exp(heights), shape[position] // blocks).reshape((-1,) + (1,) * (len(shape) - 1 - position))
    return factor_of


def scatter_about(key, extent, deviation, reach, shards=(), held_as=jnp.bfloat16):
    result = deviation * jax.random.normal(key, extent, jnp.float32)
    if shards:
        result = result * steps_of(key, extent, shards, -0.22, 0.18)
    return jnp.clip(result, -reach, reach).astype(held_as)


def setup_inputs(seed: int = 0) -> dict:
    splits = jax.random.split(jax.random.key(seed), 6)
    return {
        "populations": draw_populations(jax.random.fold_in(splits[5], 71), 0),
        "adjoint_seed": scatter_about(splits[1], (Q, NX, NY, NZ), 1.0, 6.0, ((1, 16), (2, 4), (3, 4)), jnp.float32),
        "wall_slip": jnp.clip(0.1 + 0.79999997 * jax.random.uniform(splits[2], (NX, NY, NZ), jnp.float32) ** steps_of(splits[2], (NX, NY, NZ), ((0, 16), (1, 4), (2, 4)), -0.2, 0.2), 0.1, 0.9),
        "permeability": jnp.clip(0.2 + 0.75 * jax.random.uniform(splits[3], (NX, NY, NZ), jnp.float32) ** steps_of(splits[3], (NX, NY, NZ), ((0, 16), (1, 4), (2, 4)), -0.2, 0.2), 0.2, 0.95),
        "cell_kinds": touch_ends(jax.random.randint(splits[4], (NX, NY, NZ), 0, 3), jax.random.fold_in(splits[4], 1), 0, 2).astype(jnp.int32),
    }


VELOCITY = np.array([[0, 0, 0], [1, 0, 0], [-1, 0, 0], [0, 1, 0], [0, -1, 0], [0, 0, 1], [0, 0, -1], [1, 1, 0], [-1, -1, 0], [1, -1, 0], [-1, 1, 0], [1, 0, 1], [-1, 0, -1], [1, 0, -1], [-1, 0, 1], [0, 1, 1], [0, -1, -1], [0, 1, -1], [0, -1, 1]])
WEIGHT = np.array([1.0 / 3.0] + [1.0 / 18.0] * 6 + [1.0 / 36.0] * 12)
OPPOSITE = [0, 2, 1, 4, 3, 6, 5, 8, 7, 10, 9, 12, 11, 14, 13, 16, 15, 18, 17]
RELAX = 1.25

def collide(states, wall_slip, permeability, cell_kinds):
    vectors = jnp.asarray(VELOCITY, states.dtype)
    weights = jnp.asarray(WEIGHT, states.dtype).reshape(19, 1, 1, 1)
    density = lax.optimization_barrier(jnp.sum(states, axis=0))
    momentum = jnp.einsum('qa,qxyz->axyz', vectors, states, precision=lax.Precision.HIGHEST)
    damping = jnp.where(cell_kinds == 1, permeability, jnp.ones_like(permeability))
    drift = momentum * (damping / density)[None]
    projected = jnp.einsum('qa,axyz->qxyz', vectors, drift, precision=lax.Precision.HIGHEST)
    speed_sq = lax.optimization_barrier(jnp.sum(drift * drift, axis=0))
    equilibrium = weights * density[None] * (1.0 + 3.0 * projected + 4.5 * projected * projected - 1.5 * speed_sq[None])
    relaxed = states - RELAX * (states - equilibrium)
    bounced = jnp.stack([states[other] for other in OPPOSITE])
    walled = wall_slip[None] * relaxed + (1.0 - wall_slip[None]) * bounced
    return jnp.where((cell_kinds == 2)[None], walled, relaxed)

def stream(states):
    moved = [jnp.roll(states[which], tuple((int(v) for v in VELOCITY[which])), axis=(0, 1, 2)) for which in range(19)]
    return jnp.stack(moved)

def advance(states, wall_slip, permeability, cell_kinds):
    first = stream(collide(states, wall_slip, permeability, cell_kinds))
    return stream(collide(first, wall_slip, permeability, cell_kinds))

def reference(populations, adjoint_seed, wall_slip, permeability, cell_kinds):

    def loss_map(states, slip_field, perm_field):
        return advance(states, slip_field, perm_field, cell_kinds)
    _, pullback = jax.vjp(loss_map, populations, wall_slip, permeability)
    grad_states, grad_slip, grad_perm = pullback(adjoint_seed)
    return (grad_states, grad_slip, grad_perm)
```

```python
import jax
import jax.numpy as jnp
from jax import lax
from jax.experimental import pallas as pl
from jax.experimental.pallas import tpu as pltpu
from jax.sharding import PartitionSpec as P

MESH = pl.DeviceIdType.MESH
VELOCITY = (
    (0, 0, 0), (1, 0, 0), (-1, 0, 0), (0, 1, 0), (0, -1, 0), (0, 0, 1), (0, 0, -1),
    (1, 1, 0), (-1, -1, 0), (1, -1, 0), (-1, 1, 0), (1, 0, 1), (-1, 0, -1),
    (1, 0, -1), (-1, 0, 1), (0, 1, 1), (0, -1, -1), (0, 1, -1), (0, -1, 1),
)
OPPOSITE = (0, 2, 1, 4, 3, 6, 5, 8, 7, 10, 9, 12, 11, 14, 13, 16, 15, 18, 17)
ORDER = (1, 7, 9, 11, 13, 2, 8, 10, 12, 14, 3, 4, 5, 6, 15, 16, 17, 18, 0)
SLOT = {v: s for s, v in enumerate(ORDER)}
ALONG_Y = ((3, 7, 10, 15, 17), (4, 8, 9, 16, 18))
ALONG_Z = ((5, 11, 14, 15, 18), (6, 12, 13, 16, 17))
W0, W1, W2 = 1.0 / 3.0, 1.0 / 18.0, 1.0 / 36.0
X, Y, Z = 8, 8, 128
BASE = 16
ROWS = 96


def lane_of(k, x):
    return 16 * k + x + 1


def pairs_of(f):
    plus = {i: f[i] + f[i + 1] for i in range(1, 19, 2)}
    minus = {i: f[i] - f[i + 1] for i in range(1, 19, 2)}
    return plus, minus


def vector_of(m):
    return (
        m[1] + ((m[7] + m[9]) + (m[11] + m[13])),
        m[3] + ((m[7] - m[9]) + (m[15] + m[17])),
        m[5] + ((m[11] - m[13]) + (m[15] - m[17])),
    )


def along(i, u):
    total = None
    for c, part in zip(VELOCITY[i], u):
        if c:
            part = part if c > 0 else -part
            total = part if total is None else total + part
    return total


def macroscopic(f, damping):
    plus, minus = pairs_of(f)
    rho = f[0]
    diagonal = (plus[7] + plus[9]) + (plus[11] + plus[13]) + (plus[15] + plus[17])
    rho = rho + ((plus[1] + plus[3]) + (plus[5] + diagonal))
    m = vector_of(minus)
    k = damping / rho
    u = tuple(part * k for part in m)
    usq = u[0] * u[0] + u[1] * u[1] + u[2] * u[2]
    return plus, minus, rho, m, u, usq


def coefficients(slip, perm, kind):
    wall = kind == 2
    keep = jnp.where(wall, slip, 1.0)
    bounce = jnp.where(wall, 1.0 - slip, 0.0)
    damping = jnp.where(kind == 1, perm, 1.0)
    even = 0.5 * bounce - 0.125 * keep
    odd = -0.5 * bounce - 0.125 * keep
    return keep, damping, even, odd


def collide(f, slip, perm, kind):
    keep, damping, even, odd = coefficients(slip, perm, kind)
    plus, minus, rho, m, u, usq = macroscopic(f, damping)
    scale = 1.25 * keep * rho
    base = 1.0 - 1.5 * usq
    out = {0: 2.0 * even * f[0] + W0 * scale * base}
    s1, s2 = W1 * scale, W2 * scale
    s1_base, s2_base = s1 * base, s2 * base
    for i in range(1, 19, 2):
        s, sb = (s1, s1_base) if i < 7 else (s2, s2_base)
        p = along(i, u)
        sp = s * p
        e = sb + 4.5 * (sp * p) + even * plus[i]
        o = 3.0 * sp + odd * minus[i]
        out[i] = e + o
        out[i + 1] = e - o
    return out


def pull(f, g, slip, perm, kind):
    keep, damping, even, odd = coefficients(slip, perm, kind)
    plus, minus, rho, m, u, usq = macroscopic(f, damping)
    gp, gm = pairs_of(g)
    w1g = {i: W1 * gp[i] for i in (1, 3, 5)}
    s_xy, s_xz, s_yz = gp[7] + gp[9], gp[11] + gp[13], gp[15] + gp[17]
    a0 = W0 * g[0] + W1 * (gp[1] + gp[3] + gp[5]) + W2 * (s_xy + s_xz + s_yz)
    b = (
        W1 * gm[1] + W2 * ((gm[7] + gm[9]) + (gm[11] + gm[13])),
        W1 * gm[3] + W2 * ((gm[7] - gm[9]) + (gm[15] + gm[17])),
        W1 * gm[5] + W2 * ((gm[11] - gm[13]) + (gm[15] - gm[17])),
    )
    dxx = w1g[1] + W2 * (s_xy + s_xz)
    dyy = w1g[3] + W2 * (s_xy + s_yz)
    dzz = w1g[5] + W2 * (s_xz + s_yz)
    dxy, dxz, dyz = W2 * (gp[7] - gp[9]), W2 * (gp[11] - gp[13]), W2 * (gp[15] - gp[17])
    du = (
        dxx * u[0] + dxy * u[1] + dxz * u[2],
        dxy * u[0] + dyy * u[1] + dyz * u[2],
        dxz * u[0] + dyz * u[1] + dzz * u[2],
    )
    udu = u[0] * du[0] + u[1] * du[1] + u[2] * du[2]
    ub = u[0] * b[0] + u[1] * b[1] + u[2] * b[2]
    v = tuple(b[i] + 3.0 * du[i] - a0 * u[i] for i in range(3))
    a0usq = a0 * usq
    g_rho = 1.25 * keep * (a0 + 1.5 * a0usq - 4.5 * udu)
    factor = 3.75 * keep * damping
    g_m = tuple(factor * part for part in v)
    out = {0: 2.0 * even * g[0] + g_rho}
    sum_plus, sum_minus = None, None
    for i in range(1, 19, 2):
        s = even * gp[i] + g_rho
        t = odd * gm[i] + along(i, g_m)
        out[i] = s + t
        out[i + 1] = s - t
        a, c = gp[i] * plus[i], gm[i] * minus[i]
        sum_plus = a if sum_plus is None else sum_plus + a
        sum_minus = c if sum_minus is None else sum_minus + c
    of_wall = (
        0.375 * sum_minus
        - 0.625 * sum_plus
        - 1.25 * (g[0] * f[0])
        + 1.25 * rho * (a0 - 1.5 * a0usq + 3.0 * ub + 4.5 * udu)
    )
    of_porous = 3.75 * (v[0] * m[0] + v[1] * m[1] + v[2] * m[2])
    return out, jnp.where(kind == 2, of_wall, 0.0), jnp.where(kind == 1, of_porous, 0.0)


def kernel(
    pop_hbm, seed_hbm, slip_hbm, perm_hbm, kind_hbm,
    gpop_hbm, gslip_hbm, gperm_hbm,
    pops, out, slip, perm, kind, gslip, gperm, fields, ysend, zsend, yrecv, zrecv,
    load_sem, store_sem, send_sem, recv_sem,
):
    here = tuple(lax.axis_index(a) for a in ("gx", "gy", "gz"))
    sizes = tuple(lax.axis_size(a) for a in ("gx", "gy", "gz"))

    def device(*steps):
        return tuple(
            lax.rem(h + (s + n), n) if s else h for h, s, n in zip(here, steps, sizes)
        )

    neighbours = [c for c in VELOCITY if any(c)]
    col, seed, grad = 0, 1, 2

    load_seed = [
        pltpu.make_async_copy(
            seed_hbm.at[i],
            fields.at[seed, SLOT[OPPOSITE[i]], pl.ds(BASE, X * Y), :],
            load_sem.at[i],
        )
        for i in range(19)
    ]
    for c in load_seed:
        c.start()
    load_rest = [
        pltpu.make_async_copy(src, dst, load_sem.at[19 + n])
        for n, (src, dst) in enumerate(
            ((pop_hbm, pops), (slip_hbm, slip), (perm_hbm, perm), (kind_hbm, kind))
        )
    ]
    for c in load_rest:
        c.start()

    barrier = pltpu.get_barrier_semaphore()
    for c in neighbours:
        pl.semaphore_signal(barrier, inc=1, device_id=device(*c), device_id_type=MESH)

    lane = lax.broadcasted_iota(jnp.int32, (Y, Z), 1)
    row = lax.broadcasted_iota(jnp.int32, (Y, Z), 0)

    def pack_z(values, x, packed):
        up, down = packed
        for k, v in enumerate(ALONG_Z[0]):
            at = lane_of(k, x)
            up = jnp.where(lane == at, pltpu.roll(values(v), at + 1, 1), up)
        for k, v in enumerate(ALONG_Z[1]):
            at = lane_of(k, x)
            down = jnp.where(lane == at, pltpu.roll(values(v), at, 1), down)
        return up, down

    nothing = jnp.zeros((Y, Z), jnp.float32)

    def pack_y(field):
        for side, first in ((0, BASE + Y - 1), (1, BASE)):
            for k, v in enumerate(ALONG_Y[side]):
                ysend[field, side, k] = fields[field, SLOT[v], pl.ds(first, X, stride=Y), :]

    def sends(field):
        def copy(src, dst, steps):
            return pltpu.make_async_remote_copy(
                src_ref=src, dst_ref=dst, send_sem=send_sem.at[field], recv_sem=recv_sem.at[field],
                device_id=device(*steps), device_id_type=MESH,
            )

        buf = fields.at[field]
        last = BASE + (X - 1) * Y
        copies = [
            copy(buf.at[pl.ds(0, 5), pl.ds(last, Y), :], buf.at[pl.ds(0, 5), pl.ds(BASE - Y, Y), :], (1, 0, 0)),
            copy(buf.at[pl.ds(5, 5), pl.ds(BASE, Y), :], buf.at[pl.ds(5, 5), pl.ds(last + Y, Y), :], (-1, 0, 0)),
        ]
        for side, sz in ((0, 1), (1, -1)):
            src = zsend.at[field, side]
            for place, steps in enumerate(((0, 0, sz), (1, 0, sz), (-1, 0, sz), (0, 1, sz), (0, -1, sz))):
                copies.append(copy(src, zrecv.at[field, side, place], steps))
        for side, sy in ((0, 1), (1, -1)):
            copies.append(
                copy(ysend.at[field, side], yrecv.at[field, side, :, pl.ds(Y, X), :], (0, sy, 0))
            )
            for k, v in enumerate(ALONG_Y[side]):
                cx = VELOCITY[v][0]
                if cx:
                    at = 0 if cx > 0 else 2 * Y
                    copies.append(
                        copy(ysend.at[field, side, k], yrecv.at[field, side, k, pl.ds(at, Y), :], (cx, sy, 0))
                    )
        for c in copies:
            c.start()

    def wait_all(sem):
        rows = pops.at[pl.ds(0, 17), pl.ds(0, 2 * Y), :]
        pltpu.make_async_copy(rows, rows, sem).wait()

    def assemble_z(field):
        tiles = []
        for side in range(2):
            face, left, right, below, above = (zrecv[field, side, n] for n in range(5))
            tile = face
            for k, v in enumerate(ALONG_Z[side]):
                cx, cy, _ = VELOCITY[v]
                if cx > 0:
                    tile = jnp.where(lane == lane_of(k, -1), pltpu.roll(left, Z - X, 1), tile)
                if cx < 0:
                    tile = jnp.where(lane == lane_of(k, X), pltpu.roll(right, X, 1), tile)
                group = (lane >= 16 * k) & (lane < 16 * k + 16)
                if cy > 0:
                    moved = pltpu.roll(jnp.where(row == Y - 1, below, face), 1, 0)
                    tile = jnp.where(group, moved, tile)
                if cy < 0:
                    moved = pltpu.roll(jnp.where(row == 0, above, face), Y - 1, 0)
                    tile = jnp.where(group, moved, tile)
            tiles.append(tile)
        return tiles

    def streamed(field, x, tiles):
        result = {}
        for v in range(19):
            cx, cy, cz = VELOCITY[v]
            at = BASE + Y * (x - cx)
            if cy == 0:
                value = fields[field, SLOT[v], pl.ds(pl.multiple_of(at, Y), Y), :]
            else:
                side = 0 if cy > 0 else 1
                k = ALONG_Y[side].index(v)
                value = fields[field, SLOT[v], pl.ds(at - cy, Y), :]
                halo = yrecv[field, side, k, pl.ds(Y + x - cx, 1), :]
                value = jnp.where(row == (0 if cy > 0 else Y - 1), halo, value)
            if cz > 0:
                at = lane_of(ALONG_Z[0].index(v), x - cx)
                value = jnp.where(lane == 0, pltpu.roll(tiles[0], Z - at, 1), pltpu.roll(value, 1, 1))
            if cz < 0:
                at = lane_of(ALONG_Z[1].index(v), x - cx)
                value = jnp.where(lane == Z - 1, pltpu.roll(tiles[1], Z - 1 - at, 1), pltpu.roll(value, Z - 1, 1))
            result[v] = value
        return result

    def put(field, x, values):
        at = pl.multiple_of(BASE + Y * x, Y)
        for v in range(19):
            fields[field, SLOT[v], pl.ds(at, Y), :] = values[v]

    def plane(ref, x):
        return ref[:, pl.ds(pl.multiple_of(Y * x, Y), Y), :]

    for c in load_seed:
        c.wait()

    def pack_seed(x, packed):
        at = pl.multiple_of(BASE + Y * x, Y)
        return pack_z(lambda v: fields[seed, SLOT[v], pl.ds(at, Y), :], x, packed)

    up, down = lax.fori_loop(0, X, pack_seed, (nothing, nothing))
    zsend[seed, 0], zsend[seed, 1] = up, down
    pack_y(seed)
    pl.semaphore_wait(barrier, len(neighbours))
    sends(seed)

    for c in load_rest:
        c.wait()

    def first(x, packed):
        f = {v: pops[v, pl.ds(pl.multiple_of(Y * x, Y), Y), :] for v in range(19)}
        collided = collide(f, slip[x], perm[x], kind[x])
        put(col, x, collided)
        return pack_z(lambda v: collided[v], x, packed)

    up, down = lax.fori_loop(0, X, first, (nothing, nothing))
    zsend[col, 0], zsend[col, 1] = up, down
    pack_y(col)
    sends(col)

    wait_all(recv_sem.at[seed])
    wait_all(recv_sem.at[col])
    tiles_seed, tiles_col = assemble_z(seed), assemble_z(col)

    def second(x, packed):
        f = streamed(col, x, tiles_col)
        moved = streamed(seed, x, tiles_seed)
        g = {i: moved[OPPOSITE[i]] for i in range(19)}
        result, of_slip, of_perm = pull(f, g, slip[x], perm[x], kind[x])
        gslip[x], gperm[x] = of_slip, of_perm
        turned = {OPPOSITE[i]: result[i] for i in range(19)}
        put(grad, x, turned)
        return pack_z(lambda v: turned[v], x, packed)

    up, down = lax.fori_loop(0, X, second, (nothing, nothing))
    zsend[grad, 0], zsend[grad, 1] = up, down
    pack_y(grad)
    sends(grad)

    wait_all(recv_sem.at[grad])
    tiles_grad = assemble_z(grad)

    def third(x, carry):
        f = {v: pops[v, pl.ds(pl.multiple_of(Y * x, Y), Y), :] for v in range(19)}
        moved = streamed(grad, x, tiles_grad)
        g = {i: moved[OPPOSITE[i]] for i in range(19)}
        result, of_slip, of_perm = pull(f, g, slip[x], perm[x], kind[x])
        for v in range(19):
            out[v, x] = result[v]
        gslip[x] = gslip[x] + of_slip
        gperm[x] = gperm[x] + of_perm
        return carry

    lax.fori_loop(0, X, third, 0)
    stores = [
        pltpu.make_async_copy(src, dst, store_sem.at[n])
        for n, (src, dst) in enumerate(((out, gpop_hbm), (gslip, gslip_hbm), (gperm, gperm_hbm)))
    ]
    for c in stores:
        c.start()
    for c in stores:
        c.wait()
    for field in (seed, col, grad):
        wait_all(send_sem.at[field])


def body(populations, adjoint_seed, wall_slip, permeability, cell_kinds):
    f32 = jnp.float32
    anywhere = pl.BlockSpec(memory_space=pl.ANY)
    call = pl.pallas_call(
        kernel,
        out_shape=(
            jax.ShapeDtypeStruct((19, X, Y, Z), f32),
            jax.ShapeDtypeStruct((X, Y, Z), f32),
            jax.ShapeDtypeStruct((X, Y, Z), f32),
        ),
        in_specs=[anywhere] * 5,
        out_specs=(anywhere,) * 3,
        scratch_shapes=[
            pltpu.VMEM((19, X * Y, Z), f32),
            pltpu.VMEM((19, X, Y, Z), f32),
            pltpu.VMEM((X, Y, Z), f32),
            pltpu.VMEM((X, Y, Z), f32),
            pltpu.VMEM((X, Y, Z), jnp.int32),
            pltpu.VMEM((X, Y, Z), f32),
            pltpu.VMEM((X, Y, Z), f32),
            pltpu.VMEM((3, 19, ROWS, Z), f32),
            pltpu.VMEM((3, 2, 5, X, Z), f32),
            pltpu.VMEM((3, 2, Y, Z), f32),
            pltpu.VMEM((3, 2, 5, 3 * Y, Z), f32),
            pltpu.VMEM((3, 2, 5, Y, Z), f32),
            pltpu.SemaphoreType.DMA((23,)),
            pltpu.SemaphoreType.DMA((3,)),
            pltpu.SemaphoreType.DMA((3,)),
            pltpu.SemaphoreType.DMA((3,)),
        ],
        compiler_params=pltpu.CompilerParams(
            collective_id=0, has_side_effects=True, vmem_limit_bytes=16 * 1024 * 1024
        ),
    )
    return call(
        populations.reshape(19, X * Y, Z),
        adjoint_seed.reshape(19, X * Y, Z),
        wall_slip,
        permeability,
        cell_kinds,
    )


def solution(mesh):
    state, field = P(None, "gx", "gy", "gz"), P("gx", "gy", "gz")
    return jax.shard_map(
        body,
        mesh=mesh,
        in_specs=(state, state, field, field, field),
        out_specs=(state, field, field),
        check_vma=False,
    )
```

```python
import jax
import jax.numpy as jnp
from jax import lax
from jax.experimental import pallas as pl
from jax.experimental.pallas import tpu as pltpu
from jax.sharding import PartitionSpec as P

MESH = pl.DeviceIdType.MESH
VELOCITY = (
    (0, 0, 0), (1, 0, 0), (-1, 0, 0), (0, 1, 0), (0, -1, 0), (0, 0, 1), (0, 0, -1),
    (1, 1, 0), (-1, -1, 0), (1, -1, 0), (-1, 1, 0), (1, 0, 1), (-1, 0, -1),
    (1, 0, -1), (-1, 0, 1), (0, 1, 1), (0, -1, -1), (0, 1, -1), (0, -1, 1),
)
OPPOSITE = (0, 2, 1, 4, 3, 6, 5, 8, 7, 10, 9, 12, 11, 14, 13, 16, 15, 18, 17)
ORDER = (1, 7, 9, 11, 13, 2, 8, 10, 12, 14, 3, 4, 5, 6, 15, 16, 17, 18, 0)
SLOT = {v: s for s, v in enumerate(ORDER)}
ALONG_Y = ((3, 7, 10, 15, 17), (4, 8, 9, 16, 18))
ALONG_Z = ((5, 11, 14, 15, 18), (6, 12, 13, 16, 17))
W0, W1, W2 = 1.0 / 3.0, 1.0 / 18.0, 1.0 / 36.0
X, Y, Z = 8, 8, 128
BASE = 8
ROWS = 80


def lane_of(k, x):
    return 16 * k + x + 1


def pairs_of(f):
    plus = {i: f[i] + f[i + 1] for i in range(1, 19, 2)}
    minus = {i: f[i] - f[i + 1] for i in range(1, 19, 2)}
    return plus, minus


def vector_of(m):
    return (
        m[1] + ((m[7] + m[9]) + (m[11] + m[13])),
        m[3] + ((m[7] - m[9]) + (m[15] + m[17])),
        m[5] + ((m[11] - m[13]) + (m[15] - m[17])),
    )


def along(i, u):
    total = None
    for c, part in zip(VELOCITY[i], u):
        if c:
            part = part if c > 0 else -part
            total = part if total is None else total + part
    return total


def macroscopic(f, damping):
    plus, minus = pairs_of(f)
    rho = f[0]
    diagonal = (plus[7] + plus[9]) + (plus[11] + plus[13]) + (plus[15] + plus[17])
    rho = rho + ((plus[1] + plus[3]) + (plus[5] + diagonal))
    m = vector_of(minus)
    k = damping / rho
    u = tuple(part * k for part in m)
    usq = u[0] * u[0] + u[1] * u[1] + u[2] * u[2]
    return plus, minus, rho, m, u, usq


def coefficients(slip, perm, kind):
    wall = kind == 2
    keep = jnp.where(wall, slip, 1.0)
    bounce = jnp.where(wall, 1.0 - slip, 0.0)
    damping = jnp.where(kind == 1, perm, 1.0)
    even = 0.5 * bounce - 0.125 * keep
    odd = -0.5 * bounce - 0.125 * keep
    return keep, damping, even, odd


def collide(f, slip, perm, kind):
    keep, damping, even, odd = coefficients(slip, perm, kind)
    plus, minus, rho, m, u, usq = macroscopic(f, damping)
    scale = 1.25 * keep * rho
    base = 1.0 - 1.5 * usq
    out = {0: 2.0 * even * f[0] + W0 * scale * base}
    s1, s2 = W1 * scale, W2 * scale
    s1_base, s2_base = s1 * base, s2 * base
    for i in range(1, 19, 2):
        s, sb = (s1, s1_base) if i < 7 else (s2, s2_base)
        p = along(i, u)
        sp = s * p
        e = sb + 4.5 * (sp * p) + even * plus[i]
        o = 3.0 * sp + odd * minus[i]
        out[i] = e + o
        out[i + 1] = e - o
    return out


def pull(f, g, slip, perm, kind):
    keep, damping, even, odd = coefficients(slip, perm, kind)
    plus, minus, rho, m, u, usq = macroscopic(f, damping)
    gp, gm = pairs_of(g)
    w1g = {i: W1 * gp[i] for i in (1, 3, 5)}
    s_xy, s_xz, s_yz = gp[7] + gp[9], gp[11] + gp[13], gp[15] + gp[17]
    a0 = W0 * g[0] + W1 * (gp[1] + gp[3] + gp[5]) + W2 * (s_xy + s_xz + s_yz)
    b = (
        W1 * gm[1] + W2 * ((gm[7] + gm[9]) + (gm[11] + gm[13])),
        W1 * gm[3] + W2 * ((gm[7] - gm[9]) + (gm[15] + gm[17])),
        W1 * gm[5] + W2 * ((gm[11] - gm[13]) + (gm[15] - gm[17])),
    )
    dxx = w1g[1] + W2 * (s_xy + s_xz)
    dyy = w1g[3] + W2 * (s_xy + s_yz)
    dzz = w1g[5] + W2 * (s_xz + s_yz)
    dxy, dxz, dyz = W2 * (gp[7] - gp[9]), W2 * (gp[11] - gp[13]), W2 * (gp[15] - gp[17])
    du = (
        dxx * u[0] + dxy * u[1] + dxz * u[2],
        dxy * u[0] + dyy * u[1] + dyz * u[2],
        dxz * u[0] + dyz * u[1] + dzz * u[2],
    )
    udu = u[0] * du[0] + u[1] * du[1] + u[2] * du[2]
    ub = u[0] * b[0] + u[1] * b[1] + u[2] * b[2]
    v = tuple(b[i] + 3.0 * du[i] - a0 * u[i] for i in range(3))
    a0usq = a0 * usq
    g_rho = 1.25 * keep * (a0 + 1.5 * a0usq - 4.5 * udu)
    factor = 3.75 * keep * damping
    g_m = tuple(factor * part for part in v)
    out = {0: 2.0 * even * g[0] + g_rho}
    sum_plus, sum_minus = None, None
    for i in range(1, 19, 2):
        s = even * gp[i] + g_rho
        t = odd * gm[i] + along(i, g_m)
        out[i] = s + t
        out[i + 1] = s - t
        a, c = gp[i] * plus[i], gm[i] * minus[i]
        sum_plus = a if sum_plus is None else sum_plus + a
        sum_minus = c if sum_minus is None else sum_minus + c
    of_wall = (
        0.375 * sum_minus
        - 0.625 * sum_plus
        - 1.25 * (g[0] * f[0])
        + 1.25 * rho * (a0 - 1.5 * a0usq + 3.0 * ub + 4.5 * udu)
    )
    of_porous = 3.75 * (v[0] * m[0] + v[1] * m[1] + v[2] * m[2])
    return out, jnp.where(kind == 2, of_wall, 0.0), jnp.where(kind == 1, of_porous, 0.0)


def kernel(
    pop_hbm, seed_hbm, slip_hbm, perm_hbm, kind_hbm,
    out, gslip, gperm,
    pops, slip, perm, kind, fields, ysend, zsend, xrecv, yrecv, zrecv, xyrecv, xzrecv, yzrecv,
    load_sem, send_sem, recv_sem,
):
    here = tuple(lax.axis_index(a) for a in ("gx", "gy", "gz"))
    sizes = tuple(lax.axis_size(a) for a in ("gx", "gy", "gz"))

    def device(steps):
        return tuple(
            lax.rem(h + (s + n), n) if s else h for h, s, n in zip(here, steps, sizes)
        )

    neighbours = sorted((c for c in VELOCITY if any(c)), key=lambda c: (-abs(c[0]), -sum(map(abs, c))))
    col, seed, grad = 0, 1, 2

    barrier = pltpu.get_barrier_semaphore()
    for c in neighbours:
        pl.semaphore_signal(barrier, inc=1, device_id=device(c), device_id_type=MESH)

    load_rest = [
        pltpu.make_async_copy(src, dst, load_sem.at[19 + n])
        for n, (src, dst) in enumerate(
            ((pop_hbm, pops), (slip_hbm, slip), (perm_hbm, perm), (kind_hbm, kind))
        )
    ]
    load_seed = [
        pltpu.make_async_copy(
            seed_hbm.at[i],
            fields.at[seed, SLOT[OPPOSITE[i]], pl.ds(BASE, X * Y), :],
            load_sem.at[i],
        )
        for i in range(19)
    ]
    for c in load_rest + load_seed:
        c.start()

    lane = lax.broadcasted_iota(jnp.int32, (Y, Z), 1)
    row = lax.broadcasted_iota(jnp.int32, (Y, Z), 0)

    def pack_z(values, x, packed):
        up, down = packed
        for k, v in enumerate(ALONG_Z[0]):
            at = lane_of(k, x)
            up = jnp.where(lane == at, pltpu.roll(values(v), at + 1, 1), up)
        for k, v in enumerate(ALONG_Z[1]):
            at = lane_of(k, x)
            down = jnp.where(lane == at, pltpu.roll(values(v), at, 1), down)
        return up, down

    nothing = jnp.zeros((Y, Z), jnp.float32)

    def pack_y(field):
        for side, first in ((0, BASE + Y - 1), (1, BASE)):
            for k, v in enumerate(ALONG_Y[side]):
                ysend[field, side, k] = fields[field, SLOT[v], pl.ds(first, X, stride=Y), :]

    def copies_of(which, turn):
        def copy(src, dst, steps):
            n = 2 * turn + (0 if steps[0] else 1)
            return pltpu.make_async_remote_copy(
                src_ref=src, dst_ref=dst, send_sem=send_sem.at[n], recv_sem=recv_sem.at[n],
                device_id=device(steps), device_id_type=MESH,
            )

        far, near = [], []
        last = BASE + (X - 1) * Y
        for side, (at, cx) in enumerate(((last, 1), (BASE, -1))):
            far.append(copy(
                fields.at[which, pl.ds(5 * side, 5), pl.ds(at, Y), :],
                xrecv.at[which, side, :, pl.ds(Y, Y), :], (cx, 0, 0),
            ))
        for side, cy in ((0, 1), (1, -1)):
            for k, v in enumerate(ALONG_Y[side]):
                cx = VELOCITY[v][0]
                if cx:
                    x = X - 1 if cx > 0 else 0
                    far.append(copy(
                        ysend.at[which, side, k, pl.ds(x, 1), :],
                        xyrecv.at[which, side, 0 if cx > 0 else 1], (cx, cy, 0),
                    ))
            near.append(copy(ysend.at[which, side], yrecv.at[which, side], (0, cy, 0)))
        for side, cz in ((0, 1), (1, -1)):
            src = zsend.at[which, side]
            for n, c in enumerate((1, -1)):
                far.append(copy(src, xzrecv.at[which, side, n], (c, 0, cz)))
                near.append(copy(src, yzrecv.at[which, side, n], (0, c, cz)))
            near.append(copy(src, zrecv.at[which, side], (0, 0, cz)))
        return far, near

    def wait_all(sem, rows):
        depth = 58 if rows % 58 == 0 else 64
        some = pops.at[pl.ds(0, rows // depth), pl.ds(0, depth), :]
        pltpu.make_async_copy(some, some, sem).wait()

    def near_tiles(field):
        tiles = []
        for side in range(2):
            face = zrecv[field, side]
            tile = face
            for k, v in enumerate(ALONG_Z[side]):
                cy = VELOCITY[v][1]
                group = (lane >= 16 * k) & (lane < 16 * k + 16)
                if cy > 0:
                    moved = pltpu.roll(jnp.where(row == Y - 1, yzrecv[field, side, 0], face), 1, 0)
                    tile = jnp.where(group, moved, tile)
                if cy < 0:
                    moved = pltpu.roll(jnp.where(row == 0, yzrecv[field, side, 1], face), Y - 1, 0)
                    tile = jnp.where(group, moved, tile)
            tiles.append(tile)
        return tiles

    def all_tiles(field, tiles):
        result = []
        for side, tile in enumerate(tiles):
            for k, v in enumerate(ALONG_Z[side]):
                cx = VELOCITY[v][0]
                if cx > 0:
                    tile = jnp.where(lane == lane_of(k, -1), pltpu.roll(xzrecv[field, side, 0], Z - X, 1), tile)
                if cx < 0:
                    tile = jnp.where(lane == lane_of(k, X), pltpu.roll(xzrecv[field, side, 1], X, 1), tile)
            result.append(tile)
        return result

    def streamed(field, x, tiles):
        result = {}
        for v in range(19):
            cx, cy, cz = VELOCITY[v]
            outside = isinstance(x, int) and not 0 <= x - cx < X
            if outside:
                end = 0 if cx > 0 else 1
                value = xrecv[field, end, SLOT[v] - 5 * end, pl.ds(Y - cy, Y), :]
            elif cy:
                value = fields[field, SLOT[v], pl.ds(BASE + Y * (x - cx) - cy, Y), :]
            else:
                value = fields[field, SLOT[v], pl.ds(pl.multiple_of(BASE + Y * (x - cx), Y), Y), :]
            if cy:
                side = 0 if cy > 0 else 1
                if outside:
                    halo = xyrecv[field, side, end]
                else:
                    halo = yrecv[field, side, ALONG_Y[side].index(v), pl.ds(x - cx, 1), :]
                value = jnp.where(row == (0 if cy > 0 else Y - 1), halo, value)
            if cz > 0:
                at = lane_of(ALONG_Z[0].index(v), x - cx)
                value = jnp.where(lane == 0, pltpu.roll(tiles[0], Z - at, 1), pltpu.roll(value, 1, 1))
            if cz < 0:
                at = lane_of(ALONG_Z[1].index(v), x - cx)
                value = jnp.where(lane == Z - 1, pltpu.roll(tiles[1], Z - 1 - at, 1), pltpu.roll(value, Z - 1, 1))
            result[v] = value
        return result

    def put(field, x, values):
        at = pl.multiple_of(BASE + Y * x, Y)
        for v in range(19):
            fields[field, SLOT[v], pl.ds(at, Y), :] = values[v]

    def start(copies):
        for c in copies:
            c.start()

    for c in load_seed:
        c.wait()

    def pack_seed(x, packed):
        at = pl.multiple_of(BASE + Y * x, Y)
        return pack_z(lambda v: fields[seed, SLOT[v], pl.ds(at, Y), :], x, packed)

    up, down = lax.fori_loop(0, X, pack_seed, (nothing, nothing))
    zsend[seed, 0], zsend[seed, 1] = up, down
    pack_y(seed)

    for c in load_rest:
        c.wait()

    def first(x, packed):
        f = {v: pops[v, pl.ds(pl.multiple_of(Y * x, Y), Y), :] for v in range(19)}
        collided = collide(f, slip[x], perm[x], kind[x])
        put(col, x, collided)
        return pack_z(lambda v: collided[v], x, packed)

    up, down = lax.fori_loop(0, X, first, (nothing, nothing))
    zsend[col, 0], zsend[col, 1] = up, down
    pack_y(col)

    both = pl.ds(0, 2)
    pl.semaphore_wait(barrier, len(neighbours))
    far, near = copies_of(both, 0)
    start(far + near)

    def second(x, packed, tiles_col, tiles_seed):
        f = streamed(col, x, tiles_col)
        moved = streamed(seed, x, tiles_seed)
        g = {i: moved[OPPOSITE[i]] for i in range(19)}
        result, of_slip, of_perm = pull(f, g, slip[x], perm[x], kind[x])
        gslip[x], gperm[x] = of_slip, of_perm
        turned = {OPPOSITE[i]: result[i] for i in range(19)}
        put(grad, x, turned)
        return pack_z(lambda v: turned[v], x, packed)

    FAR, NEAR = 2 * 5 * Y + 4 + 4 * Y, 2 * 5 * Y + 6 * Y
    wait_all(recv_sem.at[1], 2 * NEAR)
    tiles_col, tiles_seed = near_tiles(col), near_tiles(seed)
    packed = lax.fori_loop(1, X - 1, lambda x, p: second(x, p, tiles_col, tiles_seed), (nothing, nothing))
    wait_all(recv_sem.at[0], 2 * FAR)
    tiles_col, tiles_seed = all_tiles(col, tiles_col), all_tiles(seed, tiles_seed)
    for x in (0, X - 1):
        packed = second(x, packed, tiles_col, tiles_seed)
    zsend[grad, 0], zsend[grad, 1] = packed
    pack_y(grad)
    far, near = copies_of(grad, 1)
    start(far + near)

    def third(x, tiles):
        f = {v: pops[v, pl.ds(pl.multiple_of(Y * x, Y), Y), :] for v in range(19)}
        moved = streamed(grad, x, tiles)
        g = {i: moved[OPPOSITE[i]] for i in range(19)}
        result, of_slip, of_perm = pull(f, g, slip[x], perm[x], kind[x])
        for v in range(19):
            out[v, x] = result[v]
        gslip[x] = gslip[x] + of_slip
        gperm[x] = gperm[x] + of_perm

    def inner(x, carry):
        third(x, tiles)
        return carry

    wait_all(recv_sem.at[3], NEAR)
    tiles = near_tiles(grad)
    lax.fori_loop(1, X - 1, inner, 0)
    for n, rows in ((0, 2 * FAR), (1, 2 * NEAR), (3, NEAR)):
        wait_all(send_sem.at[n], rows)
    wait_all(recv_sem.at[2], FAR)
    tiles = all_tiles(grad, tiles)
    for x in (0, X - 1):
        third(x, tiles)
    wait_all(send_sem.at[2], FAR)


def store(out, gslip, gperm, out_hbm, gslip_hbm, gperm_hbm, sem):
    copies = [
        pltpu.make_async_copy(src, dst, sem.at[n])
        for n, (src, dst) in enumerate(((out, out_hbm), (gslip, gslip_hbm), (gperm, gperm_hbm)))
    ]
    for c in copies:
        c.start()
    for c in copies:
        c.wait()


def body(populations, adjoint_seed, wall_slip, permeability, cell_kinds):
    f32 = jnp.float32
    hbm = pl.BlockSpec(memory_space=pltpu.HBM)
    resident = pl.BlockSpec(memory_space=pltpu.VMEM)
    shapes = ((19, X, Y, Z), (X, Y, Z), (X, Y, Z))
    call = pl.pallas_call(
        kernel,
        out_shape=tuple(pltpu.VMEM(shape, f32) for shape in shapes),
        in_specs=[hbm] * 5,
        out_specs=(resident,) * 3,
        scratch_shapes=[
            pltpu.VMEM((19, X * Y, Z), f32),
            pltpu.VMEM((X, Y, Z), f32),
            pltpu.VMEM((X, Y, Z), f32),
            pltpu.VMEM((X, Y, Z), jnp.int32),
            pltpu.VMEM((3, 19, ROWS, Z), f32),
            pltpu.VMEM((3, 2, 5, X, Z), f32),
            pltpu.VMEM((3, 2, Y, Z), f32),
            pltpu.VMEM((3, 2, 5, 3 * Y, Z), f32),
            pltpu.VMEM((3, 2, 5, X, Z), f32),
            pltpu.VMEM((3, 2, Y, Z), f32),
            pltpu.VMEM((3, 2, 2, 1, Z), f32),
            pltpu.VMEM((3, 2, 2, Y, Z), f32),
            pltpu.VMEM((3, 2, 2, Y, Z), f32),
            pltpu.SemaphoreType.DMA((23,)),
            pltpu.SemaphoreType.DMA((4,)),
            pltpu.SemaphoreType.DMA((4,)),
        ],
        compiler_params=pltpu.CompilerParams(
            collective_id=0, has_side_effects=True, vmem_limit_bytes=16 * 1024 * 1024
        ),
    )
    operands = (
        populations.reshape(19, X * Y, Z),
        adjoint_seed.reshape(19, X * Y, Z),
        wall_slip,
        permeability,
        cell_kinds,
    )
    results = call(*(pltpu.with_memory_space_constraint(a, pltpu.HBM) for a in operands))
    return pl.pallas_call(
        store,
        out_shape=tuple(jax.ShapeDtypeStruct(shape, f32) for shape in shapes),
        in_specs=[resident] * 3,
        out_specs=(hbm,) * 3,
        scratch_shapes=[pltpu.SemaphoreType.DMA((3,))],
        compiler_params=pltpu.CompilerParams(vmem_limit_bytes=1024 * 1024),
    )(*(pltpu.with_memory_space_constraint(a, pltpu.VMEM) for a in results))


def solution(mesh):
    state, field = P(None, "gx", "gy", "gz"), P("gx", "gy", "gz")
    return jax.shard_map(
        body,
        mesh=mesh,
        in_specs=(state, state, field, field, field),
        out_specs=(state, field, field),
        check_vma=False,
    )
```

```python
import jax
import jax.numpy as jnp
from jax import lax
from jax.experimental import pallas as pl
from jax.experimental.pallas import tpu as pltpu
from jax.sharding import PartitionSpec as P

MESH = pl.DeviceIdType.MESH
VELOCITY = (
    (0, 0, 0), (1, 0, 0), (-1, 0, 0), (0, 1, 0), (0, -1, 0), (0, 0, 1), (0, 0, -1),
    (1, 1, 0), (-1, -1, 0), (1, -1, 0), (-1, 1, 0), (1, 0, 1), (-1, 0, -1),
    (1, 0, -1), (-1, 0, 1), (0, 1, 1), (0, -1, -1), (0, 1, -1), (0, -1, 1),
)
OPPOSITE = (0, 2, 1, 4, 3, 6, 5, 8, 7, 10, 9, 12, 11, 14, 13, 16, 15, 18, 17)
ORDER = (1, 7, 9, 11, 13, 2, 8, 10, 12, 14, 3, 4, 5, 6, 15, 16, 17, 18, 0)
SLOT = {v: s for s, v in enumerate(ORDER)}
ALONG_Y = ((3, 7, 10, 15, 17), (4, 8, 9, 16, 18))
ALONG_Z = ((5, 11, 14, 15, 18), (6, 12, 13, 16, 17))
W0, W1, W2 = 1.0 / 3.0, 1.0 / 18.0, 1.0 / 36.0
X, Y, Z = 8, 8, 128
BASE = 8
ROWS = 80


def lane_of(group, x):
    return 10 * group + x + 1


def pairs_of(f):
    plus = {i: f[i] + f[i + 1] for i in range(1, 19, 2)}
    minus = {i: f[i] - f[i + 1] for i in range(1, 19, 2)}
    return plus, minus


def vector_of(m):
    return (
        m[1] + ((m[7] + m[9]) + (m[11] + m[13])),
        m[3] + ((m[7] - m[9]) + (m[15] + m[17])),
        m[5] + ((m[11] - m[13]) + (m[15] - m[17])),
    )


def along(i, u):
    total = None
    for c, part in zip(VELOCITY[i], u):
        if c:
            part = part if c > 0 else -part
            total = part if total is None else total + part
    return total


def macroscopic(f, damping):
    plus, minus = pairs_of(f)
    rho = f[0]
    diagonal = (plus[7] + plus[9]) + (plus[11] + plus[13]) + (plus[15] + plus[17])
    rho = rho + ((plus[1] + plus[3]) + (plus[5] + diagonal))
    m = vector_of(minus)
    k = damping / rho
    u = tuple(part * k for part in m)
    usq = u[0] * u[0] + u[1] * u[1] + u[2] * u[2]
    return plus, minus, rho, m, u, usq


def coefficients(slip, perm, kind):
    wall = kind == 2
    keep = jnp.where(wall, slip, 1.0)
    bounce = jnp.where(wall, 1.0 - slip, 0.0)
    damping = jnp.where(kind == 1, perm, 1.0)
    even = 0.5 * bounce - 0.125 * keep
    odd = -0.5 * bounce - 0.125 * keep
    return keep, damping, even, odd


def collide(f, slip, perm, kind):
    keep, damping, even, odd = coefficients(slip, perm, kind)
    plus, minus, rho, m, u, usq = macroscopic(f, damping)
    scale = 1.25 * keep * rho
    base = 1.0 - 1.5 * usq
    out = {0: 2.0 * even * f[0] + W0 * scale * base}
    s1, s2 = W1 * scale, W2 * scale
    s1_base, s2_base = s1 * base, s2 * base
    for i in range(1, 19, 2):
        s, sb = (s1, s1_base) if i < 7 else (s2, s2_base)
        p = along(i, u)
        sp = s * p
        e = sb + 4.5 * (sp * p) + even * plus[i]
        o = 3.0 * sp + odd * minus[i]
        out[i] = e + o
        out[i + 1] = e - o
    return out


def pull(f, g, slip, perm, kind):
    keep, damping, even, odd = coefficients(slip, perm, kind)
    plus, minus, rho, m, u, usq = macroscopic(f, damping)
    gp, gm = pairs_of(g)
    w1g = {i: W1 * gp[i] for i in (1, 3, 5)}
    s_xy, s_xz, s_yz = gp[7] + gp[9], gp[11] + gp[13], gp[15] + gp[17]
    a0 = W0 * g[0] + W1 * (gp[1] + gp[3] + gp[5]) + W2 * (s_xy + s_xz + s_yz)
    b = (
        W1 * gm[1] + W2 * ((gm[7] + gm[9]) + (gm[11] + gm[13])),
        W1 * gm[3] + W2 * ((gm[7] - gm[9]) + (gm[15] + gm[17])),
        W1 * gm[5] + W2 * ((gm[11] - gm[13]) + (gm[15] - gm[17])),
    )
    dxx = w1g[1] + W2 * (s_xy + s_xz)
    dyy = w1g[3] + W2 * (s_xy + s_yz)
    dzz = w1g[5] + W2 * (s_xz + s_yz)
    dxy, dxz, dyz = W2 * (gp[7] - gp[9]), W2 * (gp[11] - gp[13]), W2 * (gp[15] - gp[17])
    du = (
        dxx * u[0] + dxy * u[1] + dxz * u[2],
        dxy * u[0] + dyy * u[1] + dyz * u[2],
        dxz * u[0] + dyz * u[1] + dzz * u[2],
    )
    udu = u[0] * du[0] + u[1] * du[1] + u[2] * du[2]
    ub = u[0] * b[0] + u[1] * b[1] + u[2] * b[2]
    v = tuple(b[i] + 3.0 * du[i] - a0 * u[i] for i in range(3))
    a0usq = a0 * usq
    g_rho = 1.25 * keep * (a0 + 1.5 * a0usq - 4.5 * udu)
    factor = 3.75 * keep * damping
    g_m = tuple(factor * part for part in v)
    out = {0: 2.0 * even * g[0] + g_rho}
    sum_plus, sum_minus = None, None
    for i in range(1, 19, 2):
        s = even * gp[i] + g_rho
        t = odd * gm[i] + along(i, g_m)
        out[i] = s + t
        out[i + 1] = s - t
        a, c = gp[i] * plus[i], gm[i] * minus[i]
        sum_plus = a if sum_plus is None else sum_plus + a
        sum_minus = c if sum_minus is None else sum_minus + c
    of_wall = (
        0.375 * sum_minus
        - 0.625 * sum_plus
        - 1.25 * (g[0] * f[0])
        + 1.25 * rho * (a0 - 1.5 * a0usq + 3.0 * ub + 4.5 * udu)
    )
    of_porous = 3.75 * (v[0] * m[0] + v[1] * m[1] + v[2] * m[2])
    return out, jnp.where(kind == 2, of_wall, 0.0), jnp.where(kind == 1, of_porous, 0.0)


def kernel(
    pop_hbm, seed_hbm, slip_hbm, perm_hbm, kind_hbm,
    out, gslip, gperm,
    pops, slip, perm, kind, fields, ysend, zsend, xrecv, yrecv, zrecv, xyrecv, xzrecv, yzrecv,
    load_sem, send_sem, recv_sem,
):
    here = tuple(lax.axis_index(a) for a in ("gx", "gy", "gz"))
    sizes = tuple(lax.axis_size(a) for a in ("gx", "gy", "gz"))

    def device(steps):
        return tuple(
            lax.rem(h + (s + n), n) if s else h for h, s, n in zip(here, steps, sizes)
        )

    neighbours = sorted((c for c in VELOCITY if any(c)), key=lambda c: (-abs(c[0]), -abs(c[1]), -sum(map(abs, c))))
    col, seed, grad = 0, 1, 2

    barrier = pltpu.get_barrier_semaphore()
    for c in neighbours:
        pl.semaphore_signal(barrier, inc=1, device_id=device(c), device_id_type=MESH)

    load_rest = [
        pltpu.make_async_copy(src, dst, load_sem.at[19 + n])
        for n, (src, dst) in enumerate(
            ((pop_hbm, pops), (slip_hbm, slip), (perm_hbm, perm), (kind_hbm, kind))
        )
    ]
    load_seed = [
        pltpu.make_async_copy(
            seed_hbm.at[i],
            fields.at[seed, SLOT[OPPOSITE[i]], pl.ds(BASE, X * Y), :],
            load_sem.at[i],
        )
        for i in range(19)
    ]
    for c in load_rest + load_seed:
        c.start()

    lane = lax.broadcasted_iota(jnp.int32, (Y, Z), 1)
    row = lax.broadcasted_iota(jnp.int32, (Y, Z), 0)

    def pack_z(values, x, packed, member):
        up, down = packed
        for k, v in enumerate(ALONG_Z[0]):
            at = lane_of(5 * member + k, x)
            up = jnp.where(lane == at, pltpu.roll(values(v), at + 1, 1), up)
        for k, v in enumerate(ALONG_Z[1]):
            at = lane_of(5 * member + k, x)
            down = jnp.where(lane == at, pltpu.roll(values(v), at, 1), down)
        return up, down

    nothing = jnp.zeros((Y, Z), jnp.float32)

    def pack_y(field):
        for side, first in ((0, BASE + Y - 1), (1, BASE)):
            for k, v in enumerate(ALONG_Y[side]):
                ysend[field, side, k] = fields[field, SLOT[v], pl.ds(first, X, stride=Y), :]

    def copy(src, dst, steps, n):
        return pltpu.make_async_remote_copy(
            src_ref=src, dst_ref=dst, send_sem=send_sem.at[n], recv_sem=recv_sem.at[n],
            device_id=device(steps), device_id_type=MESH,
        )

    def diagonals(which):
        for side, cy in ((0, 1), (1, -1)):
            for k, v in enumerate(ALONG_Y[side]):
                cx = VELOCITY[v][0]
                if cx:
                    src = ysend.at[which, side, k, pl.ds(X - 1 if cx > 0 else 0, 1), :]
                    yield src, (which, side, 0 if cx > 0 else 1), cx, cy

    def copies_of(which, turn):
        xs, xz, near = [], [], []
        FAR, NEAR = 2 * turn, 2 * turn + 1
        last = BASE + (X - 1) * Y
        for side, (at, cx) in enumerate(((last, 1), (BASE, -1))):
            xs.append(copy(
                fields.at[which, pl.ds(5 * side, 5), pl.ds(at, Y), :],
                xrecv.at[which, side, :, pl.ds(Y, Y), :], (cx, 0, 0), FAR,
            ))
        for side, cy in ((0, 1), (1, -1)):
            near.append(copy(ysend.at[which, side], yrecv.at[which, side], (0, cy, 0), NEAR))
        for side, cz in ((0, 1), (1, -1)):
            tile = zsend.at[turn, side]
            near.append(copy(tile, zrecv.at[turn, side], (0, 0, cz), NEAR))
            for n, c in enumerate((1, -1)):
                xz.append(copy(tile, xzrecv.at[turn, side, n], (c, 0, cz), FAR))
                end = zsend.at[turn, side, pl.ds(Y - 1 if c > 0 else 0, 1), :]
                near.append(copy(end, yzrecv.at[turn, side, n], (0, c, cz), NEAR))
        return xs, xz, near

    def wait_all(sem, rows):
        depth = next(d for d in (58, 50, 60, 8) if rows % d == 0)
        some = pops.at[pl.ds(0, rows // depth), pl.ds(0, depth), :]
        pltpu.make_async_copy(some, some, sem).wait()

    def lanes(turn, side, wanted, xs):
        mask = None
        for group in range(10 if turn == 0 else 5):
            if wanted(VELOCITY[ALONG_Z[side][group % 5]]):
                a, b = lane_of(group, xs[0]), lane_of(group, xs[1])
                here = (lane >= a) & (lane <= b)
                mask = here if mask is None else mask | here
        return mask

    def near_tiles(turn):
        tiles = []
        for side in range(2):
            face = zrecv[turn, side]
            up = jnp.where(row == 0, yzrecv[turn, side, 0], pltpu.roll(face, 1, 0))
            down = jnp.where(row == Y - 1, yzrecv[turn, side, 1], pltpu.roll(face, Y - 1, 0))
            tile = jnp.where(lanes(turn, side, lambda c: c[1] > 0, (-1, X)), up, face)
            tiles.append(jnp.where(lanes(turn, side, lambda c: c[1] < 0, (-1, X)), down, tile))
        return tiles

    def all_tiles(turn, tiles):
        result = []
        for side, tile in enumerate(tiles):
            left = pltpu.roll(xzrecv[turn, side, 0], Z - X, 1)
            right = pltpu.roll(xzrecv[turn, side, 1], X, 1)
            tile = jnp.where(lanes(turn, side, lambda c: c[0] > 0, (-1, -1)), left, tile)
            result.append(jnp.where(lanes(turn, side, lambda c: c[0] < 0, (X, X)), right, tile))
        return result

    def streamed(field, x, tiles, member):
        result = {}
        for v in range(19):
            cx, cy, cz = VELOCITY[v]
            outside = isinstance(x, int) and not 0 <= x - cx < X
            if outside:
                end = 0 if cx > 0 else 1
                value = xrecv[field, end, SLOT[v] - 5 * end, pl.ds(Y - cy, Y), :]
            elif cy:
                value = fields[field, SLOT[v], pl.ds(BASE + Y * (x - cx) - cy, Y), :]
            else:
                value = fields[field, SLOT[v], pl.ds(pl.multiple_of(BASE + Y * (x - cx), Y), Y), :]
            if cy:
                side = 0 if cy > 0 else 1
                if outside:
                    halo = xyrecv[field, side, end]
                else:
                    halo = yrecv[field, side, ALONG_Y[side].index(v), pl.ds(x - cx, 1), :]
                value = jnp.where(row == (0 if cy > 0 else Y - 1), halo, value)
            if cz > 0:
                at = lane_of(5 * member + ALONG_Z[0].index(v), x - cx)
                value = jnp.where(lane == 0, pltpu.roll(tiles[0], Z - at, 1), pltpu.roll(value, 1, 1))
            if cz < 0:
                at = lane_of(5 * member + ALONG_Z[1].index(v), x - cx)
                value = jnp.where(lane == Z - 1, pltpu.roll(tiles[1], Z - 1 - at, 1), pltpu.roll(value, Z - 1, 1))
            result[v] = value
        return result

    def put(field, x, values):
        at = pl.multiple_of(BASE + Y * x, Y)
        for v in range(19):
            fields[field, SLOT[v], pl.ds(at, Y), :] = values[v]

    def start(copies):
        for c in copies:
            c.start()

    for c in load_seed:
        c.wait()

    def pack_seed(x, packed):
        at = pl.multiple_of(BASE + Y * x, Y)
        return pack_z(lambda v: fields[seed, SLOT[v], pl.ds(at, Y), :], x, packed, 1)

    packed = lax.fori_loop(0, X, pack_seed, (nothing, nothing))
    pack_y(seed)

    for c in load_rest:
        c.wait()

    def first(x, packed):
        f = {v: pops[v, pl.ds(pl.multiple_of(Y * x, Y), Y), :] for v in range(19)}
        collided = collide(f, slip[x], perm[x], kind[x])
        put(col, x, collided)
        return pack_z(lambda v: collided[v], x, packed, 0)

    zsend[0, 0], zsend[0, 1] = lax.fori_loop(0, X, first, packed)
    pack_y(col)

    both = pl.ds(0, 2)
    pl.semaphore_wait(barrier, len(neighbours))
    xs, xz, near = copies_of(both, 0)
    start([copy(src, xyrecv.at[at], (cx, cy, 0), 0) for src, at, cx, cy in diagonals(both)] + xs + xz + near)

    def second(x, packed, tiles):
        f = streamed(col, x, tiles, 0)
        moved = streamed(seed, x, tiles, 1)
        g = {i: moved[OPPOSITE[i]] for i in range(19)}
        result, of_slip, of_perm = pull(f, g, slip[x], perm[x], kind[x])
        gslip[x], gperm[x] = of_slip, of_perm
        turned = {OPPOSITE[i]: result[i] for i in range(19)}
        put(grad, x, turned)
        return pack_z(lambda v: turned[v], x, packed, 0)

    wait_all(recv_sem.at[1], 180)
    tiles = near_tiles(0)
    packed = lax.fori_loop(1, X - 1, lambda x, p: second(x, p, tiles), (nothing, nothing))
    wait_all(recv_sem.at[0], 200)
    tiles = all_tiles(0, tiles)
    for x in (0, X - 1):
        packed = second(x, packed, tiles)
    zsend[1, 0], zsend[1, 1] = packed
    pack_y(grad)
    xs, xz, near = copies_of(grad, 1)
    start([copy(src, xyrecv.at[at], (cx, cy, 0), 2) for src, at, cx, cy in diagonals(grad)] + xs + xz + near)

    def third(x, tiles):
        f = {v: pops[v, pl.ds(pl.multiple_of(Y * x, Y), Y), :] for v in range(19)}
        moved = streamed(grad, x, tiles, 0)
        g = {i: moved[OPPOSITE[i]] for i in range(19)}
        result, of_slip, of_perm = pull(f, g, slip[x], perm[x], kind[x])
        for v in range(19):
            out[v, x] = result[v]
        gslip[x] = gslip[x] + of_slip
        gperm[x] = gperm[x] + of_perm

    def inner(x, carry):
        third(x, tiles)
        return carry

    wait_all(recv_sem.at[3], 100)
    tiles = near_tiles(1)
    lax.fori_loop(1, X - 1, inner, 0)
    for n, rows in ((0, 200), (1, 180), (3, 100)):
        wait_all(send_sem.at[n], rows)
    wait_all(recv_sem.at[2], 116)
    tiles = all_tiles(1, tiles)
    for x in (0, X - 1):
        third(x, tiles)
    wait_all(send_sem.at[2], 116)


def store(out, gslip, gperm, out_hbm, gslip_hbm, gperm_hbm, sem):
    copies = [
        pltpu.make_async_copy(src, dst, sem.at[n])
        for n, (src, dst) in enumerate(((out, out_hbm), (gslip, gslip_hbm), (gperm, gperm_hbm)))
    ]
    for c in copies:
        c.start()
    for c in copies:
        c.wait()


def body(populations, adjoint_seed, wall_slip, permeability, cell_kinds):
    f32 = jnp.float32
    hbm = pl.BlockSpec(memory_space=pltpu.HBM)
    resident = pl.BlockSpec(memory_space=pltpu.VMEM)
    shapes = ((19, X, Y, Z), (X, Y, Z), (X, Y, Z))
    call = pl.pallas_call(
        kernel,
        out_shape=tuple(pltpu.VMEM(shape, f32) for shape in shapes),
        in_specs=[hbm] * 5,
        out_specs=(resident,) * 3,
        scratch_shapes=[
            pltpu.VMEM((19, X * Y, Z), f32),
            pltpu.VMEM((X, Y, Z), f32),
            pltpu.VMEM((X, Y, Z), f32),
            pltpu.VMEM((X, Y, Z), jnp.int32),
            pltpu.VMEM((3, 19, ROWS, Z), f32),
            pltpu.VMEM((3, 2, 5, X, Z), f32),
            pltpu.VMEM((2, 2, Y, Z), f32),
            pltpu.VMEM((3, 2, 5, 3 * Y, Z), f32),
            pltpu.VMEM((3, 2, 5, X, Z), f32),
            pltpu.VMEM((2, 2, Y, Z), f32),
            pltpu.VMEM((3, 2, 2, 1, Z), f32),
            pltpu.VMEM((2, 2, 2, Y, Z), f32),
            pltpu.VMEM((2, 2, 2, 1, Z), f32),
            pltpu.SemaphoreType.DMA((23,)),
            pltpu.SemaphoreType.DMA((4,)),
            pltpu.SemaphoreType.DMA((4,)),
        ],
        compiler_params=pltpu.CompilerParams(
            collective_id=0, has_side_effects=True, vmem_limit_bytes=16 * 1024 * 1024
        ),
    )
    operands = (
        populations.reshape(19, X * Y, Z),
        adjoint_seed.reshape(19, X * Y, Z),
        wall_slip,
        permeability,
        cell_kinds,
    )
    results = call(*(pltpu.with_memory_space_constraint(a, pltpu.HBM) for a in operands))
    return pl.pallas_call(
        store,
        out_shape=tuple(jax.ShapeDtypeStruct(shape, f32) for shape in shapes),
        in_specs=[resident] * 3,
        out_specs=(hbm,) * 3,
        scratch_shapes=[pltpu.SemaphoreType.DMA((3,))],
        compiler_params=pltpu.CompilerParams(vmem_limit_bytes=1024 * 1024),
    )(*(pltpu.with_memory_space_constraint(a, pltpu.VMEM) for a in results))


def solution(mesh):
    state, field = P(None, "gx", "gy", "gz"), P("gx", "gy", "gz")
    return jax.shard_map(
        body,
        mesh=mesh,
        in_specs=(state, state, field, field, field),
        out_specs=(state, field, field),
        check_vma=False,
    )
```

```python
import jax
import jax.numpy as jnp
from jax import lax
from jax.experimental import pallas as pl
from jax.experimental.pallas import tpu as pltpu
from jax.sharding import PartitionSpec as P

MESH = pl.DeviceIdType.MESH
VELOCITY = (
    (0, 0, 0), (1, 0, 0), (-1, 0, 0), (0, 1, 0), (0, -1, 0), (0, 0, 1), (0, 0, -1),
    (1, 1, 0), (-1, -1, 0), (1, -1, 0), (-1, 1, 0), (1, 0, 1), (-1, 0, -1),
    (1, 0, -1), (-1, 0, 1), (0, 1, 1), (0, -1, -1), (0, 1, -1), (0, -1, 1),
)
OPPOSITE = (0, 2, 1, 4, 3, 6, 5, 8, 7, 10, 9, 12, 11, 14, 13, 16, 15, 18, 17)
ORDER = (1, 7, 9, 11, 13, 2, 8, 10, 12, 14, 3, 4, 5, 6, 15, 16, 17, 18, 0)
SLOT = {v: s for s, v in enumerate(ORDER)}
ALONG_Y = ((3, 7, 10, 15, 17), (4, 8, 9, 16, 18))
ALONG_Z = ((5, 11, 14, 15, 18), (6, 12, 13, 16, 17))
W0, W1, W2 = 1.0 / 3.0, 1.0 / 18.0, 1.0 / 36.0
X, Y, Z = 8, 8, 128
BASE = 8
ROWS = 80


def lane_of(group, x):
    return 10 * group + x + 1


def pairs_of(f):
    plus = {i: f[i] + f[i + 1] for i in range(1, 19, 2)}
    minus = {i: f[i] - f[i + 1] for i in range(1, 19, 2)}
    return plus, minus


def vector_of(m):
    return (
        m[1] + ((m[7] + m[9]) + (m[11] + m[13])),
        m[3] + ((m[7] - m[9]) + (m[15] + m[17])),
        m[5] + ((m[11] - m[13]) + (m[15] - m[17])),
    )


def along(i, u):
    total = None
    for c, part in zip(VELOCITY[i], u):
        if c:
            part = part if c > 0 else -part
            total = part if total is None else total + part
    return total


def macroscopic(f, damping):
    plus, minus = pairs_of(f)
    rho = f[0]
    diagonal = (plus[7] + plus[9]) + (plus[11] + plus[13]) + (plus[15] + plus[17])
    rho = rho + ((plus[1] + plus[3]) + (plus[5] + diagonal))
    m = vector_of(minus)
    k = damping / rho
    u = tuple(part * k for part in m)
    usq = u[0] * u[0] + u[1] * u[1] + u[2] * u[2]
    return plus, minus, rho, m, u, usq


def coefficients(slip, perm, kind):
    wall = kind == 2
    keep = jnp.where(wall, slip, 1.0)
    bounce = jnp.where(wall, 1.0 - slip, 0.0)
    damping = jnp.where(kind == 1, perm, 1.0)
    even = 0.5 * bounce - 0.125 * keep
    odd = -0.5 * bounce - 0.125 * keep
    return keep, damping, even, odd


def collide(f, slip, perm, kind):
    keep, damping, even, odd = coefficients(slip, perm, kind)
    plus, minus, rho, m, u, usq = macroscopic(f, damping)
    scale = 1.25 * keep * rho
    base = 1.0 - 1.5 * usq
    out = {0: 2.0 * even * f[0] + W0 * scale * base}
    s1, s2 = W1 * scale, W2 * scale
    s1_base, s2_base = s1 * base, s2 * base
    for i in range(1, 19, 2):
        s, sb = (s1, s1_base) if i < 7 else (s2, s2_base)
        p = along(i, u)
        sp = s * p
        e = sb + 4.5 * (sp * p) + even * plus[i]
        o = 3.0 * sp + odd * minus[i]
        out[i] = e + o
        out[i + 1] = e - o
    return out


def pull(f, g, slip, perm, kind):
    keep, damping, even, odd = coefficients(slip, perm, kind)
    plus, minus, rho, m, u, usq = macroscopic(f, damping)
    gp, gm = pairs_of(g)
    w1g = {i: W1 * gp[i] for i in (1, 3, 5)}
    s_xy, s_xz, s_yz = gp[7] + gp[9], gp[11] + gp[13], gp[15] + gp[17]
    a0 = W0 * g[0] + W1 * (gp[1] + gp[3] + gp[5]) + W2 * (s_xy + s_xz + s_yz)
    b = (
        W1 * gm[1] + W2 * ((gm[7] + gm[9]) + (gm[11] + gm[13])),
        W1 * gm[3] + W2 * ((gm[7] - gm[9]) + (gm[15] + gm[17])),
        W1 * gm[5] + W2 * ((gm[11] - gm[13]) + (gm[15] - gm[17])),
    )
    dxx = w1g[1] + W2 * (s_xy + s_xz)
    dyy = w1g[3] + W2 * (s_xy + s_yz)
    dzz = w1g[5] + W2 * (s_xz + s_yz)
    dxy, dxz, dyz = W2 * (gp[7] - gp[9]), W2 * (gp[11] - gp[13]), W2 * (gp[15] - gp[17])
    du = (
        dxx * u[0] + dxy * u[1] + dxz * u[2],
        dxy * u[0] + dyy * u[1] + dyz * u[2],
        dxz * u[0] + dyz * u[1] + dzz * u[2],
    )
    udu = u[0] * du[0] + u[1] * du[1] + u[2] * du[2]
    ub = u[0] * b[0] + u[1] * b[1] + u[2] * b[2]
    v = tuple(b[i] + 3.0 * du[i] - a0 * u[i] for i in range(3))
    a0usq = a0 * usq
    g_rho = 1.25 * keep * (a0 + 1.5 * a0usq - 4.5 * udu)
    factor = 3.75 * keep * damping
    g_m = tuple(factor * part for part in v)
    out = {0: 2.0 * even * g[0] + g_rho}
    sum_plus, sum_minus = None, None
    for i in range(1, 19, 2):
        s = even * gp[i] + g_rho
        t = odd * gm[i] + along(i, g_m)
        out[i] = s + t
        out[i + 1] = s - t
        a, c = gp[i] * plus[i], gm[i] * minus[i]
        sum_plus = a if sum_plus is None else sum_plus + a
        sum_minus = c if sum_minus is None else sum_minus + c
    of_wall = (
        0.375 * sum_minus
        - 0.625 * sum_plus
        - 1.25 * (g[0] * f[0])
        + 1.25 * rho * (a0 - 1.5 * a0usq + 3.0 * ub + 4.5 * udu)
    )
    of_porous = 3.75 * (v[0] * m[0] + v[1] * m[1] + v[2] * m[2])
    return out, jnp.where(kind == 2, of_wall, 0.0), jnp.where(kind == 1, of_porous, 0.0)


def kernel(
    pop_hbm, seed_hbm, slip_hbm, perm_hbm, kind_hbm,
    out, gslip, gperm,
    pops, slip, perm, kind, fields, ysend, zsend, xrecv, yrecv, zrecv, xyrecv, xzrecv, yzrecv,
    load_sem, send_sem, recv_sem,
):
    here = tuple(lax.axis_index(a) for a in ("gx", "gy", "gz"))
    sizes = tuple(lax.axis_size(a) for a in ("gx", "gy", "gz"))

    above = tuple(lax.rem(h + 1, n) for h, n in zip(here, sizes))
    below = tuple(lax.rem(h + n - 1, n) for h, n in zip(here, sizes))

    def device(steps):
        return tuple((h, up, down)[s] for s, h, up, down in zip(steps, here, above, below))

    neighbours = sorted((c for c in VELOCITY if any(c)), key=lambda c: (-abs(c[0]), -abs(c[1]), -sum(map(abs, c))))
    col, seed, grad = 0, 1, 2

    barrier = pltpu.get_barrier_semaphore()
    for c in neighbours:
        pl.semaphore_signal(barrier, inc=1, device_id=device(c), device_id_type=MESH)

    load_rest = [
        pltpu.make_async_copy(src, dst, load_sem.at[19 + n])
        for n, (src, dst) in enumerate(
            ((pop_hbm, pops), (slip_hbm, slip), (perm_hbm, perm), (kind_hbm, kind))
        )
    ]
    load_seed = [
        pltpu.make_async_copy(
            seed_hbm.at[i],
            fields.at[seed, SLOT[OPPOSITE[i]], pl.ds(BASE, X * Y), :],
            load_sem.at[i],
        )
        for i in range(19)
    ]
    for c in load_rest + load_seed:
        c.start()

    lane = lax.broadcasted_iota(jnp.int32, (Y, Z), 1)
    row = lax.broadcasted_iota(jnp.int32, (Y, Z), 0)

    def pack_z(values, x, packed, member):
        up, down = packed
        for k, v in enumerate(ALONG_Z[0]):
            at = lane_of(5 * member + k, x)
            up = jnp.where(lane == at, pltpu.roll(values(v), at + 1, 1), up)
        for k, v in enumerate(ALONG_Z[1]):
            at = lane_of(5 * member + k, x)
            down = jnp.where(lane == at, pltpu.roll(values(v), at, 1), down)
        return up, down

    nothing = jnp.zeros((Y, Z), jnp.float32)

    def pack_y(field):
        for side, first in ((0, BASE + Y - 1), (1, BASE)):
            for k, v in enumerate(ALONG_Y[side]):
                ysend[field, side, k] = fields[field, SLOT[v], pl.ds(first, X, stride=Y), :]

    def copy(src, dst, steps, n):
        return pltpu.make_async_remote_copy(
            src_ref=src, dst_ref=dst, send_sem=send_sem.at[n], recv_sem=recv_sem.at[n],
            device_id=device(steps), device_id_type=MESH,
        )

    def diagonals(which):
        for side, cy in ((0, 1), (1, -1)):
            for v in ALONG_Y[side]:
                cx = VELOCITY[v][0]
                if cx:
                    at = BASE + (X - 1) * Y * (cx > 0) + (Y - 1) * (cy > 0)
                    src = fields.at[which, SLOT[v], pl.ds(at, 1), :]
                    yield src, (which, side, 0 if cx > 0 else 1), cx, cy

    def copies_of(which, turn):
        xs, xz, near = [], [], []
        FAR, NEAR = 2 * turn, 2 * turn + 1
        last = BASE + (X - 1) * Y
        for side, (at, cx) in enumerate(((last, 1), (BASE, -1))):
            xs.append(copy(
                fields.at[which, pl.ds(5 * side, 5), pl.ds(at, Y), :],
                xrecv.at[which, side, :, pl.ds(Y, Y), :], (cx, 0, 0), FAR,
            ))
        for side, cy in ((0, 1), (1, -1)):
            near.append(copy(ysend.at[which, side], yrecv.at[which, side], (0, cy, 0), NEAR))
        for side, cz in ((0, 1), (1, -1)):
            tile = zsend.at[turn, side]
            near.append(copy(tile, zrecv.at[turn, side], (0, 0, cz), NEAR))
            for n, c in enumerate((1, -1)):
                xz.append(copy(tile, xzrecv.at[turn, side, n], (c, 0, cz), FAR))
                end = zsend.at[turn, side, pl.ds(Y - 1 if c > 0 else 0, 1), :]
                near.append(copy(end, yzrecv.at[turn, side, n], (0, c, cz), NEAR))
        return xs, xz, near

    def wait_all(sem, rows):
        depth = next(d for d in (58, 50, 60, 8) if rows % d == 0)
        some = pops.at[pl.ds(0, rows // depth), pl.ds(0, depth), :]
        pltpu.make_async_copy(some, some, sem).wait()

    def lanes(turn, side, wanted, xs):
        mask = None
        for group in range(10 if turn == 0 else 5):
            if wanted(VELOCITY[ALONG_Z[side][group % 5]]):
                a, b = lane_of(group, xs[0]), lane_of(group, xs[1])
                here = (lane >= a) & (lane <= b)
                mask = here if mask is None else mask | here
        return mask

    def near_tiles(turn):
        tiles = []
        for side in range(2):
            face = zrecv[turn, side]
            up = jnp.where(row == 0, yzrecv[turn, side, 0], pltpu.roll(face, 1, 0))
            down = jnp.where(row == Y - 1, yzrecv[turn, side, 1], pltpu.roll(face, Y - 1, 0))
            tile = jnp.where(lanes(turn, side, lambda c: c[1] > 0, (-1, X)), up, face)
            tiles.append(jnp.where(lanes(turn, side, lambda c: c[1] < 0, (-1, X)), down, tile))
        return tiles

    def streamed(field, x, tiles, member, ends):
        turn = 1 if field == grad else 0
        result = {}
        for v in range(19):
            cx, cy, cz = VELOCITY[v]
            outside = not 0 <= x - cx < X
            if outside != ends:
                continue
            end = 0 if cx > 0 else 1
            if outside:
                value = xrecv[field, end, SLOT[v] - 5 * end, pl.ds(Y - cy, Y), :]
            else:
                value = fields[field, SLOT[v], pl.ds(BASE + Y * (x - cx) - cy, Y), :]
            if cy:
                side = 0 if cy > 0 else 1
                if outside:
                    halo = xyrecv[field, side, end]
                else:
                    halo = yrecv[field, side, ALONG_Y[side].index(v), pl.ds(x - cx, 1), :]
                value = jnp.where(row == (0 if cy > 0 else Y - 1), halo, value)
            if cz:
                side = 0 if cz > 0 else 1
                group = 5 * member + ALONG_Z[side].index(v)
                tile = xzrecv[turn, side, end] if outside else tiles[side]
                at = lane_of(group, (x - cx) % X)
                edge, shift = (0, 1) if cz > 0 else (Z - 1, Z - 1)
                value = jnp.where(
                    lane == edge, pltpu.roll(tile, (edge - at) % Z, 1), pltpu.roll(value, shift, 1)
                )
            result[v] = value
        return result

    def put(field, x, values):
        at = BASE + Y * x
        for v in range(19):
            fields[field, SLOT[v], pl.ds(at, Y), :] = values[v]

    def start(copies):
        for c in copies:
            c.start()

    for c in load_seed:
        c.wait()

    packed = (nothing, nothing)
    for x in range(X):
        packed = pack_z(lambda v: fields[seed, SLOT[v], pl.ds(BASE + Y * x, Y), :], x, packed, 1)
    pack_y(seed)

    for c in load_rest:
        c.wait()

    for x in range(X):
        f = {v: pops[v, pl.ds(Y * x, Y), :] for v in range(19)}
        collided = collide(f, slip[x], perm[x], kind[x])
        put(col, x, collided)
        packed = pack_z(lambda v: collided[v], x, packed, 0)
    zsend[0, 0], zsend[0, 1] = packed
    pack_y(col)

    both = pl.ds(0, 2)
    pl.semaphore_wait(barrier, len(neighbours))
    xs, xz, near = copies_of(both, 0)
    nz, ny = near[2:], near[:2]
    start([copy(src, xyrecv.at[at], (cx, cy, 0), 0) for src, at, cx, cy in diagonals(both)] + nz + xz + xs + ny)

    def inside(x, tiles):
        return streamed(col, x, tiles, 0, False), streamed(seed, x, tiles, 1, False)

    def second(x, tiles, known):
        f = known[0] | streamed(col, x, tiles, 0, True)
        moved = known[1] | streamed(seed, x, tiles, 1, True)
        g = {i: moved[OPPOSITE[i]] for i in range(19)}
        result, of_slip, of_perm = pull(f, g, slip[x], perm[x], kind[x])
        gslip[x], gperm[x] = of_slip, of_perm
        turned = {OPPOSITE[i]: result[i] for i in range(19)}
        put(grad, x, turned)
        return turned

    wait_all(recv_sem.at[1], 180)
    tiles = near_tiles(0)
    packed = (nothing, nothing)
    for x in range(1, X - 1):
        turned = second(x, tiles, inside(x, tiles))
        packed = pack_z(lambda v: turned[v], x, packed, 0)
    known = {x: inside(x, tiles) for x in (0, X - 1)}
    wait_all(recv_sem.at[0], 200)
    ends = {x: second(x, tiles, known[x]) for x in (0, X - 1)}
    xs, xz, near = copies_of(grad, 1)
    nz, ny = near[2:], near[:2]
    start([copy(src, xyrecv.at[at], (cx, cy, 0), 2) for src, at, cx, cy in diagonals(grad)] + xs)
    for x, turned in ends.items():
        packed = pack_z(lambda v: turned[v], x, packed, 0)
    zsend[1, 0], zsend[1, 1] = packed
    start(nz + xz)
    pack_y(grad)
    start(ny)

    def third(x, tiles, known):
        f = {v: pops[v, pl.ds(Y * x, Y), :] for v in range(19)}
        moved = known | streamed(grad, x, tiles, 0, True)
        g = {i: moved[OPPOSITE[i]] for i in range(19)}
        result, of_slip, of_perm = pull(f, g, slip[x], perm[x], kind[x])
        for v in range(19):
            out[v, x] = result[v]
        gslip[x] = gslip[x] + of_slip
        gperm[x] = gperm[x] + of_perm

    wait_all(recv_sem.at[3], 100)
    tiles = near_tiles(1)
    for x in range(1, X - 1):
        third(x, tiles, streamed(grad, x, tiles, 0, False))
    known = {x: streamed(grad, x, tiles, 0, False) for x in (0, X - 1)}
    for n, rows in ((0, 200), (1, 180), (3, 100)):
        wait_all(send_sem.at[n], rows)
    wait_all(recv_sem.at[2], 116)
    for x in (0, X - 1):
        third(x, tiles, known[x])
    wait_all(send_sem.at[2], 116)


def store(out, gslip, gperm, out_hbm, gslip_hbm, gperm_hbm, sem):
    copies = [
        pltpu.make_async_copy(src, dst, sem.at[n])
        for n, (src, dst) in enumerate(((out, out_hbm), (gslip, gslip_hbm), (gperm, gperm_hbm)))
    ]
    for c in copies:
        c.start()
    for c in copies:
        c.wait()


def body(populations, adjoint_seed, wall_slip, permeability, cell_kinds):
    f32 = jnp.float32
    hbm = pl.BlockSpec(memory_space=pltpu.HBM)
    resident = pl.BlockSpec(memory_space=pltpu.VMEM)
    shapes = ((19, X, Y, Z), (X, Y, Z), (X, Y, Z))
    call = pl.pallas_call(
        kernel,
        out_shape=tuple(pltpu.VMEM(shape, f32) for shape in shapes),
        in_specs=[hbm] * 5,
        out_specs=(resident,) * 3,
        scratch_shapes=[
            pltpu.VMEM((19, X * Y, Z), f32),
            pltpu.VMEM((X, Y, Z), f32),
            pltpu.VMEM((X, Y, Z), f32),
            pltpu.VMEM((X, Y, Z), jnp.int32),
            pltpu.VMEM((3, 19, ROWS, Z), f32),
            pltpu.VMEM((3, 2, 5, X, Z), f32),
            pltpu.VMEM((2, 2, Y, Z), f32),
            pltpu.VMEM((3, 2, 5, 3 * Y, Z), f32),
            pltpu.VMEM((3, 2, 5, X, Z), f32),
            pltpu.VMEM((2, 2, Y, Z), f32),
            pltpu.VMEM((3, 2, 2, 1, Z), f32),
            pltpu.VMEM((2, 2, 2, Y, Z), f32),
            pltpu.VMEM((2, 2, 2, 1, Z), f32),
            pltpu.SemaphoreType.DMA((23,)),
            pltpu.SemaphoreType.DMA((4,)),
            pltpu.SemaphoreType.DMA((4,)),
        ],
        compiler_params=pltpu.CompilerParams(
            collective_id=0, has_side_effects=True, vmem_limit_bytes=16 * 1024 * 1024
        ),
    )
    operands = (
        populations.reshape(19, X * Y, Z),
        adjoint_seed.reshape(19, X * Y, Z),
        wall_slip,
        permeability,
        cell_kinds,
    )
    results = call(*(pltpu.with_memory_space_constraint(a, pltpu.HBM) for a in operands))
    return pl.pallas_call(
        store,
        out_shape=tuple(jax.ShapeDtypeStruct(shape, f32) for shape in shapes),
        in_specs=[resident] * 3,
        out_specs=(hbm,) * 3,
        scratch_shapes=[pltpu.SemaphoreType.DMA((3,))],
        compiler_params=pltpu.CompilerParams(vmem_limit_bytes=1024 * 1024),
    )(*(pltpu.with_memory_space_constraint(a, pltpu.VMEM) for a in results))


def solution(mesh):
    state, field = P(None, "gx", "gy", "gz"), P("gx", "gy", "gz")
    return jax.shard_map(
        body,
        mesh=mesh,
        in_specs=(state, state, field, field, field),
        out_specs=(state, field, field),
        check_vma=False,
    )
```

```python
import jax
import jax.numpy as jnp
from jax import lax
from jax.experimental import pallas as pl
from jax.experimental.pallas import tpu as pltpu
from jax.sharding import PartitionSpec as P

MESH = pl.DeviceIdType.MESH
VELOCITY = (
    (0, 0, 0), (1, 0, 0), (-1, 0, 0), (0, 1, 0), (0, -1, 0), (0, 0, 1), (0, 0, -1),
    (1, 1, 0), (-1, -1, 0), (1, -1, 0), (-1, 1, 0), (1, 0, 1), (-1, 0, -1),
    (1, 0, -1), (-1, 0, 1), (0, 1, 1), (0, -1, -1), (0, 1, -1), (0, -1, 1),
)
OPPOSITE = (0, 2, 1, 4, 3, 6, 5, 8, 7, 10, 9, 12, 11, 14, 13, 16, 15, 18, 17)
ORDER = (1, 7, 9, 11, 13, 2, 8, 10, 12, 14, 3, 4, 5, 6, 15, 16, 17, 18, 0)
SLOT = {v: s for s, v in enumerate(ORDER)}
ALONG_Y = ((3, 7, 10, 15, 17), (4, 8, 9, 16, 18))
ALONG_Z = ((5, 11, 14, 15, 18), (6, 12, 13, 16, 17))
W0, W1, W2 = 1.0 / 3.0, 1.0 / 18.0, 1.0 / 36.0
X, Y, Z = 8, 8, 128
BASE = 8
ROWS = 80


def lane_of(group, x):
    return 10 * group + x + 1


def pairs_of(f):
    plus = {i: f[i] + f[i + 1] for i in range(1, 19, 2)}
    minus = {i: f[i] - f[i + 1] for i in range(1, 19, 2)}
    return plus, minus


def vector_of(m):
    return (
        m[1] + ((m[7] + m[9]) + (m[11] + m[13])),
        m[3] + ((m[7] - m[9]) + (m[15] + m[17])),
        m[5] + ((m[11] - m[13]) + (m[15] - m[17])),
    )


def along(i, u):
    total = None
    for c, part in zip(VELOCITY[i], u):
        if c:
            part = part if c > 0 else -part
            total = part if total is None else total + part
    return total


def macroscopic(f, damping):
    plus, minus = pairs_of(f)
    rho = f[0]
    diagonal = (plus[7] + plus[9]) + (plus[11] + plus[13]) + (plus[15] + plus[17])
    rho = rho + ((plus[1] + plus[3]) + (plus[5] + diagonal))
    m = vector_of(minus)
    k = damping / rho
    u = tuple(part * k for part in m)
    usq = u[0] * u[0] + u[1] * u[1] + u[2] * u[2]
    return plus, minus, rho, m, u, usq


def coefficients(slip, perm, kind):
    wall = kind == 2
    keep = jnp.where(wall, slip, 1.0)
    bounce = jnp.where(wall, 1.0 - slip, 0.0)
    damping = jnp.where(kind == 1, perm, 1.0)
    even = 0.5 * bounce - 0.125 * keep
    odd = -0.5 * bounce - 0.125 * keep
    return keep, damping, even, odd


def collide(f, slip, perm, kind):
    keep, damping, even, odd = coefficients(slip, perm, kind)
    plus, minus, rho, m, u, usq = macroscopic(f, damping)
    scale = 1.25 * keep * rho
    base = 1.0 - 1.5 * usq
    out = {0: 2.0 * even * f[0] + W0 * scale * base}
    s1, s2 = W1 * scale, W2 * scale
    s1_base, s2_base = s1 * base, s2 * base
    for i in range(1, 19, 2):
        s, sb = (s1, s1_base) if i < 7 else (s2, s2_base)
        p = along(i, u)
        sp = s * p
        e = sb + 4.5 * (sp * p) + even * plus[i]
        o = 3.0 * sp + odd * minus[i]
        out[i] = e + o
        out[i + 1] = e - o
    return out


def pull(f, g, slip, perm, kind):
    keep, damping, even, odd = coefficients(slip, perm, kind)
    plus, minus, rho, m, u, usq = macroscopic(f, damping)
    gp, gm = pairs_of(g)
    w1g = {i: W1 * gp[i] for i in (1, 3, 5)}
    s_xy, s_xz, s_yz = gp[7] + gp[9], gp[11] + gp[13], gp[15] + gp[17]
    a0 = W0 * g[0] + W1 * (gp[1] + gp[3] + gp[5]) + W2 * (s_xy + s_xz + s_yz)
    b = (
        W1 * gm[1] + W2 * ((gm[7] + gm[9]) + (gm[11] + gm[13])),
        W1 * gm[3] + W2 * ((gm[7] - gm[9]) + (gm[15] + gm[17])),
        W1 * gm[5] + W2 * ((gm[11] - gm[13]) + (gm[15] - gm[17])),
    )
    dxx = w1g[1] + W2 * (s_xy + s_xz)
    dyy = w1g[3] + W2 * (s_xy + s_yz)
    dzz = w1g[5] + W2 * (s_xz + s_yz)
    dxy, dxz, dyz = W2 * (gp[7] - gp[9]), W2 * (gp[11] - gp[13]), W2 * (gp[15] - gp[17])
    du = (
        dxx * u[0] + dxy * u[1] + dxz * u[2],
        dxy * u[0] + dyy * u[1] + dyz * u[2],
        dxz * u[0] + dyz * u[1] + dzz * u[2],
    )
    udu = u[0] * du[0] + u[1] * du[1] + u[2] * du[2]
    ub = u[0] * b[0] + u[1] * b[1] + u[2] * b[2]
    v = tuple(b[i] + 3.0 * du[i] - a0 * u[i] for i in range(3))
    a0usq = a0 * usq
    g_rho = 1.25 * keep * (a0 + 1.5 * a0usq - 4.5 * udu)
    factor = 3.75 * keep * damping
    g_m = tuple(factor * part for part in v)
    out = {0: 2.0 * even * g[0] + g_rho}
    sum_plus, sum_minus = None, None
    for i in range(1, 19, 2):
        s = even * gp[i] + g_rho
        t = odd * gm[i] + along(i, g_m)
        out[i] = s + t
        out[i + 1] = s - t
        a, c = gp[i] * plus[i], gm[i] * minus[i]
        sum_plus = a if sum_plus is None else sum_plus + a
        sum_minus = c if sum_minus is None else sum_minus + c
    of_wall = (
        0.375 * sum_minus
        - 0.625 * sum_plus
        - 1.25 * (g[0] * f[0])
        + 1.25 * rho * (a0 - 1.5 * a0usq + 3.0 * ub + 4.5 * udu)
    )
    of_porous = 3.75 * (v[0] * m[0] + v[1] * m[1] + v[2] * m[2])
    return out, jnp.where(kind == 2, of_wall, 0.0), jnp.where(kind == 1, of_porous, 0.0)


def kernel(
    pop_hbm, seed_hbm, slip_hbm, perm_hbm, kind_hbm,
    out, gslip, gperm,
    pops, slip, perm, kind, fields, ysend, zsend, xrecv, yrecv, zrecv, hop, xyrecv, xzrecv, yzrecv,
    load_sem, send_sem, recv_sem,
):
    here = tuple(lax.axis_index(a) for a in ("gx", "gy", "gz"))
    sizes = tuple(lax.axis_size(a) for a in ("gx", "gy", "gz"))

    above = tuple(lax.rem(h + 1, n) for h, n in zip(here, sizes))
    below = tuple(lax.rem(h + n - 1, n) for h, n in zip(here, sizes))

    def device(steps):
        return tuple((h, up, down)[s] for s, h, up, down in zip(steps, here, above, below))

    neighbours = sorted((c for c in VELOCITY if any(c)), key=lambda c: (-abs(c[0]), -abs(c[1]), -sum(map(abs, c))))
    col, seed, grad = 0, 1, 2

    detours = (here[0] == 0) & (here[1] == 0)
    passes_on = (here[0] == sizes[0] - 1) & (here[1] == 0)

    barrier = pltpu.get_barrier_semaphore()
    for c in neighbours:
        def greet(c=c):
            pl.semaphore_signal(barrier, inc=1, device_id=device(c), device_id_type=MESH)

        if c[0] == 1 and c[1]:
            pl.when(jnp.logical_not((here[0] == sizes[0] - 1) & (device(c)[1] == 0)))(greet)
        else:
            greet()

    load_rest = [
        pltpu.make_async_copy(src, dst, load_sem.at[19 + n])
        for n, (src, dst) in enumerate(
            ((pop_hbm, pops), (slip_hbm, slip), (perm_hbm, perm), (kind_hbm, kind))
        )
    ]
    load_seed = [
        pltpu.make_async_copy(
            seed_hbm.at[i],
            fields.at[seed, SLOT[OPPOSITE[i]], pl.ds(BASE, X * Y), :],
            load_sem.at[i],
        )
        for i in range(19)
    ]
    for c in load_rest + load_seed:
        c.start()

    lane = lax.broadcasted_iota(jnp.int32, (Y, Z), 1)
    row = lax.broadcasted_iota(jnp.int32, (Y, Z), 0)

    def pack_z(values, x, packed, member):
        up, down = packed
        for k, v in enumerate(ALONG_Z[0]):
            at = lane_of(5 * member + k, x)
            up = jnp.where(lane == at, pltpu.roll(values(v), at + 1, 1), up)
        for k, v in enumerate(ALONG_Z[1]):
            at = lane_of(5 * member + k, x)
            down = jnp.where(lane == at, pltpu.roll(values(v), at, 1), down)
        return up, down

    nothing = jnp.zeros((Y, Z), jnp.float32)

    def pack_y(field):
        for side, first in ((0, BASE + Y - 1), (1, BASE)):
            for k, v in enumerate(ALONG_Y[side]):
                ysend[field, side, k] = fields[field, SLOT[v], pl.ds(first, X, stride=Y), :]

    def copy(src, dst, steps, n, arrives=None):
        arrives = n if arrives is None else arrives
        return pltpu.make_async_remote_copy(
            src_ref=src, dst_ref=dst, send_sem=send_sem.at[n], recv_sem=recv_sem.at[arrives],
            device_id=device(steps), device_id_type=MESH,
        )

    def diagonals(which):
        for side, cy in ((0, 1), (1, -1)):
            for v in ALONG_Y[side]:
                cx = VELOCITY[v][0]
                if cx:
                    at = BASE + (X - 1) * Y * (cx > 0) + (Y - 1) * (cy > 0)
                    src = fields.at[which, SLOT[v], pl.ds(at, 1), :]
                    yield src, (which, side, 0 if cx > 0 else 1), cx, cy

    def copies_of(which, turn):
        xs, xz, near = [], [], []
        FAR, NEAR = 2 * turn, 2 * turn + 1
        last = BASE + (X - 1) * Y
        for side, (at, cx) in enumerate(((last, 1), (BASE, -1))):
            xs.append(copy(
                fields.at[which, pl.ds(5 * side, 5), pl.ds(at, Y), :],
                xrecv.at[which, side, :, pl.ds(Y, Y), :], (cx, 0, 0), FAR,
            ))
        for side, cy in ((0, 1), (1, -1)):
            near.append(copy(ysend.at[which, side], yrecv.at[which, side], (0, cy, 0), NEAR))
        for side, cz in ((0, 1), (1, -1)):
            tile = zsend.at[turn, side]
            near.append(copy(tile, zrecv.at[turn, side], (0, 0, cz), NEAR))
            for n, c in enumerate((1, -1)):
                xz.append(copy(tile, xzrecv.at[turn, side, n], (c, 0, cz), FAR))
                end = zsend.at[turn, side, pl.ds(Y - 1 if c > 0 else 0, 1), :]
                near.append(copy(end, yzrecv.at[turn, side, n], (0, c, cz), NEAR))
        return xs, xz, near

    def wait_all(sem, rows):
        depth = next(d for d in (58, 50, 60, 4) if rows % d == 0)
        some = pops.at[pl.ds(0, rows // depth), pl.ds(0, depth), :]
        pltpu.make_async_copy(some, some, sem).wait()

    def lanes(turn, side, wanted, xs):
        mask = None
        for group in range(10 if turn == 0 else 5):
            if wanted(VELOCITY[ALONG_Z[side][group % 5]]):
                a, b = lane_of(group, xs[0]), lane_of(group, xs[1])
                here = (lane >= a) & (lane <= b)
                mask = here if mask is None else mask | here
        return mask

    def near_tiles(turn):
        tiles = []
        for side in range(2):
            face = zrecv[turn, side]
            up = jnp.where(row == 0, yzrecv[turn, side, 0], pltpu.roll(face, 1, 0))
            down = jnp.where(row == Y - 1, yzrecv[turn, side, 1], pltpu.roll(face, Y - 1, 0))
            tile = jnp.where(lanes(turn, side, lambda c: c[1] > 0, (-1, X)), up, face)
            tiles.append(jnp.where(lanes(turn, side, lambda c: c[1] < 0, (-1, X)), down, tile))
        return tiles

    def streamed(field, x, tiles, member, ends):
        turn = 1 if field == grad else 0
        result = {}
        for v in range(19):
            cx, cy, cz = VELOCITY[v]
            outside = not 0 <= x - cx < X
            if outside != ends:
                continue
            end = 0 if cx > 0 else 1
            if outside:
                value = xrecv[field, end, SLOT[v] - 5 * end, pl.ds(Y - cy, Y), :]
            else:
                value = fields[field, SLOT[v], pl.ds(BASE + Y * (x - cx) - cy, Y), :]
            if cy:
                side = 0 if cy > 0 else 1
                if outside:
                    halo = xyrecv[field, side, end]
                else:
                    halo = yrecv[field, side, ALONG_Y[side].index(v), pl.ds(x - cx, 1), :]
                value = jnp.where(row == (0 if cy > 0 else Y - 1), halo, value)
            if cz:
                side = 0 if cz > 0 else 1
                group = 5 * member + ALONG_Z[side].index(v)
                tile = xzrecv[turn, side, end] if outside else tiles[side]
                at = lane_of(group, (x - cx) % X)
                edge, shift = (0, 1) if cz > 0 else (Z - 1, Z - 1)
                value = jnp.where(
                    lane == edge, pltpu.roll(tile, (edge - at) % Z, 1), pltpu.roll(value, shift, 1)
                )
            result[v] = value
        return result

    def put(field, x, values):
        at = BASE + Y * x
        for v in range(19):
            fields[field, SLOT[v], pl.ds(at, Y), :] = values[v]

    def start(copies):
        for c in copies:
            c.start()

    for c in load_seed:
        c.wait()

    packed = (nothing, nothing)
    for x in range(X):
        packed = pack_z(lambda v: fields[seed, SLOT[v], pl.ds(BASE + Y * x, Y), :], x, packed, 1)
    pack_y(seed)

    for c in load_rest:
        c.wait()

    for x in range(X):
        f = {v: pops[v, pl.ds(Y * x, Y), :] for v in range(19)}
        collided = collide(f, slip[x], perm[x], kind[x])
        put(col, x, collided)
        packed = pack_z(lambda v: collided[v], x, packed, 0)
    zsend[0, 0], zsend[0, 1] = packed
    pack_y(col)

    both = pl.ds(0, 2)
    pl.semaphore_wait(barrier, len(neighbours) - 2 * detours.astype(jnp.int32))
    xs, xz, near = copies_of(both, 0)
    nz, ny = near[2:], near[:2]

    @pl.when(detours)
    def _():
        start([
            copy(src, xyrecv.at[at], (cx, cy, 0), 0) if cx > 0 else copy(src, hop.at[at[:2]], (cx, 0, 0), 0, 4)
            for src, at, cx, cy in diagonals(both)
        ])

    @pl.when(jnp.logical_not(detours))
    def _():
        start([copy(src, xyrecv.at[at], (cx, cy, 0), 0) for src, at, cx, cy in diagonals(both)])

    start(nz + xz + xs + ny)

    def inside(x, tiles):
        return streamed(col, x, tiles, 0, False), streamed(seed, x, tiles, 1, False)

    def second(x, tiles, known):
        f = known[0] | streamed(col, x, tiles, 0, True)
        moved = known[1] | streamed(seed, x, tiles, 1, True)
        g = {i: moved[OPPOSITE[i]] for i in range(19)}
        result, of_slip, of_perm = pull(f, g, slip[x], perm[x], kind[x])
        gslip[x], gperm[x] = of_slip, of_perm
        turned = {OPPOSITE[i]: result[i] for i in range(19)}
        put(grad, x, turned)
        return turned

    wait_all(recv_sem.at[1], 180)
    tiles = near_tiles(0)
    packed = (nothing, nothing)
    for x in range(1, X - 1):
        turned = second(x, tiles, inside(x, tiles))
        packed = pack_z(lambda v: turned[v], x, packed, 0)
    known = {x: inside(x, tiles) for x in (0, X - 1)}

    @pl.when(passes_on)
    def _():
        wait_all(recv_sem.at[4], 4)
        start([
            copy(hop.at[both, side], xyrecv.at[both, side, 1], (0, cy, 0), 4, 0)
            for side, cy in ((0, 1), (1, -1))
        ])

    wait_all(recv_sem.at[0], 200)
    ends = {x: second(x, tiles, known[x]) for x in (0, X - 1)}
    xs, xz, near = copies_of(grad, 1)
    nz, ny = near[2:], near[:2]
    start([copy(src, xyrecv.at[at], (cx, cy, 0), 2) for src, at, cx, cy in diagonals(grad)] + xs)
    for x, turned in ends.items():
        packed = pack_z(lambda v: turned[v], x, packed, 0)
    zsend[1, 0], zsend[1, 1] = packed
    start(nz + xz)
    pack_y(grad)
    start(ny)

    def third(x, tiles, known):
        f = {v: pops[v, pl.ds(Y * x, Y), :] for v in range(19)}
        moved = known | streamed(grad, x, tiles, 0, True)
        g = {i: moved[OPPOSITE[i]] for i in range(19)}
        result, of_slip, of_perm = pull(f, g, slip[x], perm[x], kind[x])
        for v in range(19):
            out[v, x] = result[v]
        gslip[x] = gslip[x] + of_slip
        gperm[x] = gperm[x] + of_perm

    wait_all(recv_sem.at[3], 100)
    tiles = near_tiles(1)
    for x in range(1, X - 1):
        third(x, tiles, streamed(grad, x, tiles, 0, False))
    known = {x: streamed(grad, x, tiles, 0, False) for x in (0, X - 1)}
    for n, rows in ((0, 200), (1, 180), (3, 100)):
        wait_all(send_sem.at[n], rows)

    @pl.when(passes_on)
    def _():
        wait_all(send_sem.at[4], 4)

    wait_all(recv_sem.at[2], 116)
    for x in (0, X - 1):
        third(x, tiles, known[x])
    wait_all(send_sem.at[2], 116)


def store(out, gslip, gperm, out_hbm, gslip_hbm, gperm_hbm, sem):
    copies = [
        pltpu.make_async_copy(src, dst, sem.at[n])
        for n, (src, dst) in enumerate(((out, out_hbm), (gslip, gslip_hbm), (gperm, gperm_hbm)))
    ]
    for c in copies:
        c.start()
    for c in copies:
        c.wait()


def body(populations, adjoint_seed, wall_slip, permeability, cell_kinds):
    f32 = jnp.float32
    hbm = pl.BlockSpec(memory_space=pltpu.HBM)
    resident = pl.BlockSpec(memory_space=pltpu.VMEM)
    shapes = ((19, X, Y, Z), (X, Y, Z), (X, Y, Z))
    call = pl.pallas_call(
        kernel,
        out_shape=tuple(pltpu.VMEM(shape, f32) for shape in shapes),
        in_specs=[hbm] * 5,
        out_specs=(resident,) * 3,
        scratch_shapes=[
            pltpu.VMEM((19, X * Y, Z), f32),
            pltpu.VMEM((X, Y, Z), f32),
            pltpu.VMEM((X, Y, Z), f32),
            pltpu.VMEM((X, Y, Z), jnp.int32),
            pltpu.VMEM((3, 19, ROWS, Z), f32),
            pltpu.VMEM((3, 2, 5, X, Z), f32),
            pltpu.VMEM((2, 2, Y, Z), f32),
            pltpu.VMEM((3, 2, 5, 3 * Y, Z), f32),
            pltpu.VMEM((3, 2, 5, X, Z), f32),
            pltpu.VMEM((2, 2, Y, Z), f32),
            pltpu.VMEM((2, 2, 1, Z), f32),
            pltpu.VMEM((3, 2, 2, 1, Z), f32),
            pltpu.VMEM((2, 2, 2, Y, Z), f32),
            pltpu.VMEM((2, 2, 2, 1, Z), f32),
            pltpu.SemaphoreType.DMA((23,)),
            pltpu.SemaphoreType.DMA((5,)),
            pltpu.SemaphoreType.DMA((5,)),
        ],
        compiler_params=pltpu.CompilerParams(
            collective_id=0, has_side_effects=True, vmem_limit_bytes=16 * 1024 * 1024
        ),
    )
    operands = (
        populations.reshape(19, X * Y, Z),
        adjoint_seed.reshape(19, X * Y, Z),
        wall_slip,
        permeability,
        cell_kinds,
    )
    results = call(*(pltpu.with_memory_space_constraint(a, pltpu.HBM) for a in operands))
    return pl.pallas_call(
        store,
        out_shape=tuple(jax.ShapeDtypeStruct(shape, f32) for shape in shapes),
        in_specs=[resident] * 3,
        out_specs=(hbm,) * 3,
        scratch_shapes=[pltpu.SemaphoreType.DMA((3,))],
        compiler_params=pltpu.CompilerParams(vmem_limit_bytes=1024 * 1024),
    )(*(pltpu.with_memory_space_constraint(a, pltpu.VMEM) for a in results))


def solution(mesh):
    state, field = P(None, "gx", "gy", "gz"), P("gx", "gy", "gz")
    return jax.shard_map(
        body,
        mesh=mesh,
        in_specs=(state, state, field, field, field),
        out_specs=(state, field, field),
        check_vma=False,
    )
```

```python
import functools

import jax
import jax.numpy as jnp
from jax import lax
from jax.experimental import pallas as pl
from jax.experimental.pallas import tpu as pltpu
from jax.sharding import PartitionSpec as P

MESH = pl.DeviceIdType.MESH
VELOCITY = (
    (0, 0, 0), (1, 0, 0), (-1, 0, 0), (0, 1, 0), (0, -1, 0), (0, 0, 1), (0, 0, -1),
    (1, 1, 0), (-1, -1, 0), (1, -1, 0), (-1, 1, 0), (1, 0, 1), (-1, 0, -1),
    (1, 0, -1), (-1, 0, 1), (0, 1, 1), (0, -1, -1), (0, 1, -1), (0, -1, 1),
)
OPPOSITE = (0, 2, 1, 4, 3, 6, 5, 8, 7, 10, 9, 12, 11, 14, 13, 16, 15, 18, 17)
ORDER = (1, 7, 9, 11, 13, 2, 8, 10, 12, 14, 3, 4, 5, 6, 15, 16, 17, 18, 0)
SLOT = {v: s for s, v in enumerate(ORDER)}
ALONG_Y = ((3, 7, 10, 15, 17), (4, 8, 9, 16, 18))
ALONG_Z = ((5, 11, 14, 15, 18), (6, 12, 13, 16, 17))
W0, W1, W2 = 1.0 / 3.0, 1.0 / 18.0, 1.0 / 36.0
X, Y, Z = 8, 8, 128
BASE = 8
ROWS = 80


def lane_of(group, x):
    return 10 * group + x + 1


def pairs_of(f):
    plus = {i: f[i] + f[i + 1] for i in range(1, 19, 2)}
    minus = {i: f[i] - f[i + 1] for i in range(1, 19, 2)}
    return plus, minus


def vector_of(m):
    return (
        m[1] + ((m[7] + m[9]) + (m[11] + m[13])),
        m[3] + ((m[7] - m[9]) + (m[15] + m[17])),
        m[5] + ((m[11] - m[13]) + (m[15] - m[17])),
    )


def along(i, u):
    total = None
    for c, part in zip(VELOCITY[i], u):
        if c:
            part = part if c > 0 else -part
            total = part if total is None else total + part
    return total


def macroscopic(f, damping):
    plus, minus = pairs_of(f)
    rho = f[0]
    diagonal = (plus[7] + plus[9]) + (plus[11] + plus[13]) + (plus[15] + plus[17])
    rho = rho + ((plus[1] + plus[3]) + (plus[5] + diagonal))
    m = vector_of(minus)
    k = damping / rho
    u = tuple(part * k for part in m)
    usq = u[0] * u[0] + u[1] * u[1] + u[2] * u[2]
    return plus, minus, rho, m, u, usq


def coefficients(slip, perm, kind):
    wall = kind == 2
    keep = jnp.where(wall, slip, 1.0)
    bounce = jnp.where(wall, 1.0 - slip, 0.0)
    damping = jnp.where(kind == 1, perm, 1.0)
    even = 0.5 * bounce - 0.125 * keep
    odd = -0.5 * bounce - 0.125 * keep
    return keep, damping, even, odd


def collide(f, slip, perm, kind):
    keep, damping, even, odd = coefficients(slip, perm, kind)
    plus, minus, rho, m, u, usq = macroscopic(f, damping)
    scale = 1.25 * keep * rho
    base = 1.0 - 1.5 * usq
    out = {0: 2.0 * even * f[0] + W0 * scale * base}
    s1, s2 = W1 * scale, W2 * scale
    s1_base, s2_base = s1 * base, s2 * base
    for i in range(1, 19, 2):
        s, sb = (s1, s1_base) if i < 7 else (s2, s2_base)
        p = along(i, u)
        sp = s * p
        e = sb + 4.5 * (sp * p) + even * plus[i]
        o = 3.0 * sp + odd * minus[i]
        out[i] = e + o
        out[i + 1] = e - o
    return out


def pull(f, g, slip, perm, kind):
    keep, damping, even, odd = coefficients(slip, perm, kind)
    plus, minus, rho, m, u, usq = macroscopic(f, damping)
    gp, gm = pairs_of(g)
    w1g = {i: W1 * gp[i] for i in (1, 3, 5)}
    s_xy, s_xz, s_yz = gp[7] + gp[9], gp[11] + gp[13], gp[15] + gp[17]
    a0 = W0 * g[0] + W1 * (gp[1] + gp[3] + gp[5]) + W2 * (s_xy + s_xz + s_yz)
    b = (
        W1 * gm[1] + W2 * ((gm[7] + gm[9]) + (gm[11] + gm[13])),
        W1 * gm[3] + W2 * ((gm[7] - gm[9]) + (gm[15] + gm[17])),
        W1 * gm[5] + W2 * ((gm[11] - gm[13]) + (gm[15] - gm[17])),
    )
    dxx = w1g[1] + W2 * (s_xy + s_xz)
    dyy = w1g[3] + W2 * (s_xy + s_yz)
    dzz = w1g[5] + W2 * (s_xz + s_yz)
    dxy, dxz, dyz = W2 * (gp[7] - gp[9]), W2 * (gp[11] - gp[13]), W2 * (gp[15] - gp[17])
    du = (
        dxx * u[0] + dxy * u[1] + dxz * u[2],
        dxy * u[0] + dyy * u[1] + dyz * u[2],
        dxz * u[0] + dyz * u[1] + dzz * u[2],
    )
    udu = u[0] * du[0] + u[1] * du[1] + u[2] * du[2]
    ub = u[0] * b[0] + u[1] * b[1] + u[2] * b[2]
    v = tuple(b[i] + 3.0 * du[i] - a0 * u[i] for i in range(3))
    a0usq = a0 * usq
    g_rho = 1.25 * keep * (a0 + 1.5 * a0usq - 4.5 * udu)
    factor = 3.75 * keep * damping
    g_m = tuple(factor * part for part in v)
    out = {0: 2.0 * even * g[0] + g_rho}
    sum_plus, sum_minus = None, None
    for i in range(1, 19, 2):
        s = even * gp[i] + g_rho
        t = odd * gm[i] + along(i, g_m)
        out[i] = s + t
        out[i + 1] = s - t
        a, c = gp[i] * plus[i], gm[i] * minus[i]
        sum_plus = a if sum_plus is None else sum_plus + a
        sum_minus = c if sum_minus is None else sum_minus + c
    of_wall = (
        0.375 * sum_minus
        - 0.625 * sum_plus
        - 1.25 * (g[0] * f[0])
        + 1.25 * rho * (a0 - 1.5 * a0usq + 3.0 * ub + 4.5 * udu)
    )
    of_porous = 3.75 * (v[0] * m[0] + v[1] * m[1] + v[2] * m[2])
    return out, jnp.where(kind == 2, of_wall, 0.0), jnp.where(kind == 1, of_porous, 0.0)


def kernel(
    pop_hbm, seed_hbm, slip_hbm, perm_hbm, kind_hbm,
    out, gslip, gperm,
    pops, slip, perm, kind, fields, ysend, zsend, xrecv, yrecv, zrecv, hop, xyrecv, xzrecv, yzrecv,
    load_sem, send_sem, recv_sem,
):
    here = tuple(lax.axis_index(a) for a in ("gx", "gy", "gz"))
    sizes = tuple(lax.axis_size(a) for a in ("gx", "gy", "gz"))

    above = tuple(lax.rem(h + 1, n) for h, n in zip(here, sizes))
    below = tuple(lax.rem(h + n - 1, n) for h, n in zip(here, sizes))
    col, seed, grad = 0, 1, 2

    odd = lax.rem(here[0], 2)
    ends = (1 - odd, odd)
    across = tuple(jnp.where(end == 0, above[0], below[0]) for end in ends)
    FARTHER, CLOSER = 0, 1

    def device(place, cy, cz):
        gy, gz = ((h, up, down)[c] for c, h, up, down in zip((cy, cz), here[1:], above[1:], below[1:]))
        return (here[0] if place is None else across[place], gy, gz)

    detours = (here[0] == 0) & (here[1] == 0)
    passes_on = (here[0] == sizes[0] - 1) & (here[1] == 0)

    barrier = pltpu.get_barrier_semaphore()

    def greet(target):
        pl.semaphore_signal(barrier, inc=1, device_id=target, device_id_type=MESH)

    SIDES = ((1, 0), (-1, 0)), ((0, 1), (0, -1))
    for place in (FARTHER, CLOSER):
        for cy, cz in SIDES[0]:
            if place == FARTHER:
                target = device(place, cy, cz)
                spared = (here[0] == sizes[0] - 1) & (target[1] == 0)
                pl.when(jnp.logical_not(spared))(functools.partial(greet, target))
            else:
                greet(device(place, cy, cz))
        greet(device(place, 0, 0))
        for cy, cz in SIDES[1]:
            greet(device(place, cy, cz))
    for cy in (1, -1, 0):
        for cz in (1, -1, 0):
            if cy or cz:
                greet(device(None, cy, cz))

    load_rest = [
        pltpu.make_async_copy(src, dst, load_sem.at[19 + n])
        for n, (src, dst) in enumerate(
            ((pop_hbm, pops), (slip_hbm, slip), (perm_hbm, perm), (kind_hbm, kind))
        )
    ]
    load_seed = [
        pltpu.make_async_copy(
            seed_hbm.at[i],
            fields.at[seed, SLOT[OPPOSITE[i]], pl.ds(BASE, X * Y), :],
            load_sem.at[i],
        )
        for i in range(19)
    ]
    for c in load_rest + load_seed:
        c.start()

    lane = lax.broadcasted_iota(jnp.int32, (Y, Z), 1)
    row = lax.broadcasted_iota(jnp.int32, (Y, Z), 0)

    def pack_z(values, x, packed, member):
        up, down = packed
        for k, v in enumerate(ALONG_Z[0]):
            at = lane_of(5 * member + k, x)
            up = jnp.where(lane == at, pltpu.roll(values(v), at + 1, 1), up)
        for k, v in enumerate(ALONG_Z[1]):
            at = lane_of(5 * member + k, x)
            down = jnp.where(lane == at, pltpu.roll(values(v), at, 1), down)
        return up, down

    nothing = jnp.zeros((Y, Z), jnp.float32)

    def pack_y(field):
        for side, first in ((0, BASE + Y - 1), (1, BASE)):
            for k, v in enumerate(ALONG_Y[side]):
                ysend[field, side, k] = fields[field, SLOT[v], pl.ds(first, X, stride=Y), :]

    def copy(src, dst, target, n, arrives=None):
        arrives = n if arrives is None else arrives
        return pltpu.make_async_remote_copy(
            src_ref=src, dst_ref=dst, send_sem=send_sem.at[n], recv_sem=recv_sem.at[arrives],
            device_id=target, device_id_type=MESH,
        )

    def xy_rows(which, place, n, way=None):
        end = ends[place]
        for side, cy in ((0, 1), (1, -1)):
            slot = 1 + 6 * end if cy > 0 else 2 + 4 * end
            at = BASE + (X - 1) * Y * (1 - end) + (Y - 1) * (cy > 0)
            src = fields.at[which, slot, pl.ds(at, 1), :]
            if way is None:
                yield copy(src, xyrecv.at[which, side, end], device(place, cy, 0), n)
            else:
                yield copy(src, way.at[which, side], device(place, 0, 0), n, 4)

    def x_face(which, place, n):
        end = ends[place]
        at = pl.multiple_of(BASE + (X - 1) * Y * (1 - end), Y)
        yield copy(
            fields.at[which, pl.ds(5 * end, 5), pl.ds(at, Y), :],
            xrecv.at[which, end, :, pl.ds(Y, Y), :], device(place, 0, 0), n,
        )

    def xz_tiles(turn, place, n):
        for side, cz in ((0, 1), (1, -1)):
            yield copy(zsend.at[turn, side], xzrecv.at[turn, side, ends[place]], device(place, 0, cz), n)

    def y_faces(which, n):
        for side, cy in ((0, 1), (1, -1)):
            yield copy(ysend.at[which, side], yrecv.at[which, side], device(None, cy, 0), n)

    def z_faces(turn, n):
        for side, cz in ((0, 1), (1, -1)):
            yield copy(zsend.at[turn, side], zrecv.at[turn, side], device(None, 0, cz), n)
            for k, cy in enumerate((1, -1)):
                row_of = zsend.at[turn, side, pl.ds(Y - 1 if cy > 0 else 0, 1), :]
                yield copy(row_of, yzrecv.at[turn, side, k], device(None, cy, cz), n)

    def wait_all(sem, rows):
        depth = next(d for d in (58, 50, 60, 4) if rows % d == 0)
        some = pops.at[pl.ds(0, rows // depth), pl.ds(0, depth), :]
        pltpu.make_async_copy(some, some, sem).wait()

    def lanes(turn, side, wanted, xs):
        mask = None
        for group in range(10 if turn == 0 else 5):
            if wanted(VELOCITY[ALONG_Z[side][group % 5]]):
                a, b = lane_of(group, xs[0]), lane_of(group, xs[1])
                here = (lane >= a) & (lane <= b)
                mask = here if mask is None else mask | here
        return mask

    def near_tiles(turn):
        tiles = []
        for side in range(2):
            face = zrecv[turn, side]
            up = jnp.where(row == 0, yzrecv[turn, side, 0], pltpu.roll(face, 1, 0))
            down = jnp.where(row == Y - 1, yzrecv[turn, side, 1], pltpu.roll(face, Y - 1, 0))
            tile = jnp.where(lanes(turn, side, lambda c: c[1] > 0, (-1, X)), up, face)
            tiles.append(jnp.where(lanes(turn, side, lambda c: c[1] < 0, (-1, X)), down, tile))
        return tiles

    def streamed(field, x, tiles, member, outer):
        turn = 1 if field == grad else 0
        result = {}
        for v in range(19):
            cx, cy, cz = VELOCITY[v]
            outside = not 0 <= x - cx < X
            if outside != outer:
                continue
            end = 0 if cx > 0 else 1
            if outside:
                value = xrecv[field, end, SLOT[v] - 5 * end, pl.ds(Y - cy, Y), :]
            else:
                value = fields[field, SLOT[v], pl.ds(BASE + Y * (x - cx) - cy, Y), :]
            if cy:
                side = 0 if cy > 0 else 1
                if outside:
                    halo = xyrecv[field, side, end]
                else:
                    halo = yrecv[field, side, ALONG_Y[side].index(v), pl.ds(x - cx, 1), :]
                value = jnp.where(row == (0 if cy > 0 else Y - 1), halo, value)
            if cz:
                side = 0 if cz > 0 else 1
                group = 5 * member + ALONG_Z[side].index(v)
                tile = xzrecv[turn, side, end] if outside else tiles[side]
                at = lane_of(group, (x - cx) % X)
                edge, shift = (0, 1) if cz > 0 else (Z - 1, Z - 1)
                value = jnp.where(
                    lane == edge, pltpu.roll(tile, (edge - at) % Z, 1), pltpu.roll(value, shift, 1)
                )
            result[v] = value
        return result

    def put(field, x, values):
        at = BASE + Y * x
        for v in range(19):
            fields[field, SLOT[v], pl.ds(at, Y), :] = values[v]

    def start(copies):
        for c in copies:
            c.start()

    for c in load_seed:
        c.wait()

    packed = (nothing, nothing)
    for x in range(X):
        packed = pack_z(lambda v: fields[seed, SLOT[v], pl.ds(BASE + Y * x, Y), :], x, packed, 1)
    pack_y(seed)

    for c in load_rest:
        c.wait()

    for x in range(X):
        f = {v: pops[v, pl.ds(Y * x, Y), :] for v in range(19)}
        collided = collide(f, slip[x], perm[x], kind[x])
        put(col, x, collided)
        packed = pack_z(lambda v: collided[v], x, packed, 0)
    zsend[0, 0], zsend[0, 1] = packed
    pack_y(col)

    both = pl.ds(0, 2)
    pl.semaphore_wait(barrier, 18 - 2 * detours.astype(jnp.int32))
    pl.when(detours)(lambda: start(xy_rows(both, FARTHER, 0, hop)))
    pl.when(jnp.logical_not(detours))(lambda: start(xy_rows(both, FARTHER, 0)))
    start(z_faces(0, 1))
    start(x_face(both, FARTHER, 0))
    start(xz_tiles(0, FARTHER, 0))
    start(xy_rows(both, CLOSER, 0))
    start(xz_tiles(0, CLOSER, 0))
    start(x_face(both, CLOSER, 0))
    start(y_faces(both, 1))

    def inside(x, tiles):
        return streamed(col, x, tiles, 0, False), streamed(seed, x, tiles, 1, False)

    def second(x, tiles, known):
        f = known[0] | streamed(col, x, tiles, 0, True)
        moved = known[1] | streamed(seed, x, tiles, 1, True)
        g = {i: moved[OPPOSITE[i]] for i in range(19)}
        result, of_slip, of_perm = pull(f, g, slip[x], perm[x], kind[x])
        gslip[x], gperm[x] = of_slip, of_perm
        turned = {OPPOSITE[i]: result[i] for i in range(19)}
        put(grad, x, turned)
        return turned

    wait_all(recv_sem.at[1], 180)
    tiles = near_tiles(0)
    packed = (nothing, nothing)
    for x in range(1, X - 1):
        turned = second(x, tiles, inside(x, tiles))
        packed = pack_z(lambda v: turned[v], x, packed, 0)
    known = {x: inside(x, tiles) for x in (0, X - 1)}

    @pl.when(passes_on)
    def _():
        wait_all(recv_sem.at[4], 4)
        start([
            copy(hop.at[both, side], xyrecv.at[both, side, 1], device(None, cy, 0), 4, 0)
            for side, cy in ((0, 1), (1, -1))
        ])

    wait_all(recv_sem.at[0], 200)
    outer = {x: second(x, tiles, known[x]) for x in (0, X - 1)}
    start(xy_rows(grad, FARTHER, 2))
    start(x_face(grad, FARTHER, 2))
    start(xy_rows(grad, CLOSER, 2))
    start(x_face(grad, CLOSER, 2))
    for x, turned in outer.items():
        packed = pack_z(lambda v: turned[v], x, packed, 0)
    zsend[1, 0], zsend[1, 1] = packed
    start(z_faces(1, 3))
    start(xz_tiles(1, FARTHER, 2))
    start(xz_tiles(1, CLOSER, 2))
    pack_y(grad)
    start(y_faces(grad, 3))

    def third(x, tiles, known):
        f = {v: pops[v, pl.ds(Y * x, Y), :] for v in range(19)}
        moved = known | streamed(grad, x, tiles, 0, True)
        g = {i: moved[OPPOSITE[i]] for i in range(19)}
        result, of_slip, of_perm = pull(f, g, slip[x], perm[x], kind[x])
        for v in range(19):
            out[v, x] = result[v]
        gslip[x] = gslip[x] + of_slip
        gperm[x] = gperm[x] + of_perm

    wait_all(recv_sem.at[3], 100)
    tiles = near_tiles(1)
    for x in range(1, X - 1):
        third(x, tiles, streamed(grad, x, tiles, 0, False))
    known = {x: streamed(grad, x, tiles, 0, False) for x in (0, X - 1)}
    for n, rows in ((0, 200), (1, 180), (3, 100)):
        wait_all(send_sem.at[n], rows)

    @pl.when(passes_on)
    def _():
        wait_all(send_sem.at[4], 4)

    wait_all(recv_sem.at[2], 116)
    for x in (0, X - 1):
        third(x, tiles, known[x])
    wait_all(send_sem.at[2], 116)


def store(out, gslip, gperm, out_hbm, gslip_hbm, gperm_hbm, sem):
    copies = [
        pltpu.make_async_copy(src, dst, sem.at[n])
        for n, (src, dst) in enumerate(((out, out_hbm), (gslip, gslip_hbm), (gperm, gperm_hbm)))
    ]
    for c in copies:
        c.start()
    for c in copies:
        c.wait()


def body(populations, adjoint_seed, wall_slip, permeability, cell_kinds):
    f32 = jnp.float32
    hbm = pl.BlockSpec(memory_space=pltpu.HBM)
    resident = pl.BlockSpec(memory_space=pltpu.VMEM)
    shapes = ((19, X, Y, Z), (X, Y, Z), (X, Y, Z))
    call = pl.pallas_call(
        kernel,
        out_shape=tuple(pltpu.VMEM(shape, f32) for shape in shapes),
        in_specs=[hbm] * 5,
        out_specs=(resident,) * 3,
        scratch_shapes=[
            pltpu.VMEM((19, X * Y, Z), f32),
            pltpu.VMEM((X, Y, Z), f32),
            pltpu.VMEM((X, Y, Z), f32),
            pltpu.VMEM((X, Y, Z), jnp.int32),
            pltpu.VMEM((3, 19, ROWS, Z), f32),
            pltpu.VMEM((3, 2, 5, X, Z), f32),
            pltpu.VMEM((2, 2, Y, Z), f32),
            pltpu.VMEM((3, 2, 5, 3 * Y, Z), f32),
            pltpu.VMEM((3, 2, 5, X, Z), f32),
            pltpu.VMEM((2, 2, Y, Z), f32),
            pltpu.VMEM((2, 2, 1, Z), f32),
            pltpu.VMEM((3, 2, 2, 1, Z), f32),
            pltpu.VMEM((2, 2, 2, Y, Z), f32),
            pltpu.VMEM((2, 2, 2, 1, Z), f32),
            pltpu.SemaphoreType.DMA((23,)),
            pltpu.SemaphoreType.DMA((5,)),
            pltpu.SemaphoreType.DMA((5,)),
        ],
        compiler_params=pltpu.CompilerParams(
            collective_id=0, has_side_effects=True, vmem_limit_bytes=16 * 1024 * 1024
        ),
    )
    operands = (
        populations.reshape(19, X * Y, Z),
        adjoint_seed.reshape(19, X * Y, Z),
        wall_slip,
        permeability,
        cell_kinds,
    )
    results = call(*(pltpu.with_memory_space_constraint(a, pltpu.HBM) for a in operands))
    return pl.pallas_call(
        store,
        out_shape=tuple(jax.ShapeDtypeStruct(shape, f32) for shape in shapes),
        in_specs=[resident] * 3,
        out_specs=(hbm,) * 3,
        scratch_shapes=[pltpu.SemaphoreType.DMA((3,))],
        compiler_params=pltpu.CompilerParams(vmem_limit_bytes=1024 * 1024),
    )(*(pltpu.with_memory_space_constraint(a, pltpu.VMEM) for a in results))


def solution(mesh):
    state, field = P(None, "gx", "gy", "gz"), P("gx", "gy", "gz")
    return jax.shard_map(
        body,
        mesh=mesh,
        in_specs=(state, state, field, field, field),
        out_specs=(state, field, field),
        check_vma=False,
    )
```

```python
import functools

import jax
import jax.numpy as jnp
from jax import lax
from jax.experimental import pallas as pl
from jax.experimental.pallas import tpu as pltpu
from jax.sharding import PartitionSpec as P

MESH = pl.DeviceIdType.MESH
VELOCITY = (
    (0, 0, 0), (1, 0, 0), (-1, 0, 0), (0, 1, 0), (0, -1, 0), (0, 0, 1), (0, 0, -1),
    (1, 1, 0), (-1, -1, 0), (1, -1, 0), (-1, 1, 0), (1, 0, 1), (-1, 0, -1),
    (1, 0, -1), (-1, 0, 1), (0, 1, 1), (0, -1, -1), (0, 1, -1), (0, -1, 1),
)
OPPOSITE = (0, 2, 1, 4, 3, 6, 5, 8, 7, 10, 9, 12, 11, 14, 13, 16, 15, 18, 17)
ORDER = (1, 7, 9, 11, 13, 2, 8, 10, 12, 14, 3, 4, 5, 6, 15, 16, 17, 18, 0)
SLOT = {v: s for s, v in enumerate(ORDER)}
ALONG_Y = ((3, 7, 10, 15, 17), (4, 8, 9, 16, 18))
ALONG_Z = ((5, 11, 14, 15, 18), (6, 12, 13, 16, 17))
W0, W1, W2 = 1.0 / 3.0, 1.0 / 18.0, 1.0 / 36.0
X, Y, Z = 8, 8, 128
BASE = 8
ROWS = 80


def lane_of(group, x):
    return 10 * group + x + 1


def pairs_of(f):
    plus = {i: f[i] + f[i + 1] for i in range(1, 19, 2)}
    minus = {i: f[i] - f[i + 1] for i in range(1, 19, 2)}
    return plus, minus


def vector_of(m):
    return (
        m[1] + ((m[7] + m[9]) + (m[11] + m[13])),
        m[3] + ((m[7] - m[9]) + (m[15] + m[17])),
        m[5] + ((m[11] - m[13]) + (m[15] - m[17])),
    )


def along(i, u):
    total = None
    for c, part in zip(VELOCITY[i], u):
        if c:
            part = part if c > 0 else -part
            total = part if total is None else total + part
    return total


def macroscopic(f, damping):
    plus, minus = pairs_of(f)
    rho = f[0]
    diagonal = (plus[7] + plus[9]) + (plus[11] + plus[13]) + (plus[15] + plus[17])
    rho = rho + ((plus[1] + plus[3]) + (plus[5] + diagonal))
    m = vector_of(minus)
    k = damping / rho
    u = tuple(part * k for part in m)
    usq = u[0] * u[0] + u[1] * u[1] + u[2] * u[2]
    return plus, minus, rho, m, u, usq


def coefficients(slip, perm, kind):
    wall = kind == 2
    keep = jnp.where(wall, slip, 1.0)
    bounce = jnp.where(wall, 1.0 - slip, 0.0)
    damping = jnp.where(kind == 1, perm, 1.0)
    even = 0.5 * bounce - 0.125 * keep
    odd = -0.5 * bounce - 0.125 * keep
    return keep, damping, even, odd


def collide(f, slip, perm, kind):
    keep, damping, even, odd = coefficients(slip, perm, kind)
    plus, minus, rho, m, u, usq = macroscopic(f, damping)
    scale = 1.25 * keep * rho
    base = 1.0 - 1.5 * usq
    out = {0: 2.0 * even * f[0] + W0 * scale * base}
    s1, s2 = W1 * scale, W2 * scale
    s1_base, s2_base = s1 * base, s2 * base
    for i in range(1, 19, 2):
        s, sb = (s1, s1_base) if i < 7 else (s2, s2_base)
        p = along(i, u)
        sp = s * p
        e = sb + 4.5 * (sp * p) + even * plus[i]
        o = 3.0 * sp + odd * minus[i]
        out[i] = e + o
        out[i + 1] = e - o
    return out


def pull(f, g, slip, perm, kind):
    keep, damping, even, odd = coefficients(slip, perm, kind)
    plus, minus, rho, m, u, usq = macroscopic(f, damping)
    gp, gm = pairs_of(g)
    w1g = {i: W1 * gp[i] for i in (1, 3, 5)}
    s_xy, s_xz, s_yz = gp[7] + gp[9], gp[11] + gp[13], gp[15] + gp[17]
    a0 = W0 * g[0] + W1 * (gp[1] + gp[3] + gp[5]) + W2 * (s_xy + s_xz + s_yz)
    b = (
        W1 * gm[1] + W2 * ((gm[7] + gm[9]) + (gm[11] + gm[13])),
        W1 * gm[3] + W2 * ((gm[7] - gm[9]) + (gm[15] + gm[17])),
        W1 * gm[5] + W2 * ((gm[11] - gm[13]) + (gm[15] - gm[17])),
    )
    dxx = w1g[1] + W2 * (s_xy + s_xz)
    dyy = w1g[3] + W2 * (s_xy + s_yz)
    dzz = w1g[5] + W2 * (s_xz + s_yz)
    dxy, dxz, dyz = W2 * (gp[7] - gp[9]), W2 * (gp[11] - gp[13]), W2 * (gp[15] - gp[17])
    du = (
        dxx * u[0] + dxy * u[1] + dxz * u[2],
        dxy * u[0] + dyy * u[1] + dyz * u[2],
        dxz * u[0] + dyz * u[1] + dzz * u[2],
    )
    udu = u[0] * du[0] + u[1] * du[1] + u[2] * du[2]
    ub = u[0] * b[0] + u[1] * b[1] + u[2] * b[2]
    v = tuple(b[i] + 3.0 * du[i] - a0 * u[i] for i in range(3))
    a0usq = a0 * usq
    g_rho = 1.25 * keep * (a0 + 1.5 * a0usq - 4.5 * udu)
    factor = 3.75 * keep * damping
    g_m = tuple(factor * part for part in v)
    out = {0: 2.0 * even * g[0] + g_rho}
    sum_plus, sum_minus = None, None
    for i in range(1, 19, 2):
        s = even * gp[i] + g_rho
        t = odd * gm[i] + along(i, g_m)
        out[i] = s + t
        out[i + 1] = s - t
        a, c = gp[i] * plus[i], gm[i] * minus[i]
        sum_plus = a if sum_plus is None else sum_plus + a
        sum_minus = c if sum_minus is None else sum_minus + c
    of_wall = (
        0.375 * sum_minus
        - 0.625 * sum_plus
        - 1.25 * (g[0] * f[0])
        + 1.25 * rho * (a0 - 1.5 * a0usq + 3.0 * ub + 4.5 * udu)
    )
    of_porous = 3.75 * (v[0] * m[0] + v[1] * m[1] + v[2] * m[2])
    return out, jnp.where(kind == 2, of_wall, 0.0), jnp.where(kind == 1, of_porous, 0.0)


def kernel(
    pop_hbm, seed_hbm, slip_hbm, perm_hbm, kind_hbm,
    out, gslip, gperm,
    pops, slip, perm, kind, fields, ysend, zsend, xrecv, yrecv, zrecv, hop, xyrecv, xzrecv, yzrecv,
    load_sem, send_sem, recv_sem,
):
    here = tuple(lax.axis_index(a) for a in ("gx", "gy", "gz"))
    sizes = tuple(lax.axis_size(a) for a in ("gx", "gy", "gz"))

    above = tuple(lax.rem(h + 1, n) for h, n in zip(here, sizes))
    below = tuple(lax.rem(h + n - 1, n) for h, n in zip(here, sizes))
    col, seed, grad = 0, 1, 2

    odd = lax.rem(here[0], 2)
    ends = (1 - odd, odd)
    across = tuple(jnp.where(end == 0, above[0], below[0]) for end in ends)
    FARTHER, CLOSER = 0, 1

    def device(place, cy, cz):
        gy, gz = ((h, up, down)[c] for c, h, up, down in zip((cy, cz), here[1:], above[1:], below[1:]))
        return (here[0] if place is None else across[place], gy, gz)

    phase, low = lax.rem(here[0], 4), here[1] == 0
    last = here[0] == sizes[0] - 1
    by_x, by_y = low & (here[0] == 0), low & (phase == 1)
    detours = by_x | by_y
    passes_on = low & last

    barrier = pltpu.get_barrier_semaphore()

    def greet(target):
        pl.semaphore_signal(barrier, inc=1, device_id=target, device_id_type=MESH)

    SIDES = ((1, 0), (-1, 0)), ((0, 1), (0, -1))
    for place in (FARTHER, CLOSER):
        for cy, cz in SIDES[0]:
            if place == FARTHER:
                target = device(place, cy, cz)
                spared = (last | (phase == 2)) & (target[1] == 0)
                pl.when(jnp.logical_not(spared))(functools.partial(greet, target))
            else:
                greet(device(place, cy, cz))
        for cy, cz in SIDES[1]:
            greet(device(place, cy, cz))
        greet(device(place, 0, 0))
    for cy in (1, -1, 0):
        for cz in (1, -1, 0):
            if cy or cz:
                greet(device(None, cy, cz))

    load_rest = [
        pltpu.make_async_copy(src, dst, load_sem.at[1 + n])
        for n, (src, dst) in enumerate(
            ((pop_hbm, pops), (slip_hbm, slip), (perm_hbm, perm), (kind_hbm, kind))
        )
    ]
    load_seed = [
        pltpu.make_async_copy(
            seed_hbm.at[i],
            fields.at[seed, SLOT[OPPOSITE[i]], pl.ds(BASE, X * Y), :],
            load_sem.at[0],
        )
        for i in range(19)
    ]
    for c in load_rest + load_seed:
        c.start()

    lane = lax.broadcasted_iota(jnp.int32, (Y, Z), 1)
    row = lax.broadcasted_iota(jnp.int32, (Y, Z), 0)

    def pack_z(values, x, packed, member):
        up, down = packed
        for k, v in enumerate(ALONG_Z[0]):
            at = lane_of(5 * member + k, x)
            up = jnp.where(lane == at, pltpu.roll(values(v), at + 1, 1), up)
        for k, v in enumerate(ALONG_Z[1]):
            at = lane_of(5 * member + k, x)
            down = jnp.where(lane == at, pltpu.roll(values(v), at, 1), down)
        return up, down

    nothing = jnp.zeros((Y, Z), jnp.float32)

    def pack_y(field):
        for side, first in ((0, BASE + Y - 1), (1, BASE)):
            for k, v in enumerate(ALONG_Y[side]):
                ysend[field, side, k] = fields[field, SLOT[v], pl.ds(first, X, stride=Y), :]

    def copy(src, dst, target, n, arrives=None):
        arrives = n if arrives is None else arrives
        return pltpu.make_async_remote_copy(
            src_ref=src, dst_ref=dst, send_sem=send_sem.at[n], recv_sem=recv_sem.at[arrives],
            device_id=target, device_id_type=MESH,
        )

    def xy_rows(which, place, n, way=None):
        end = ends[place]
        for side, cy in ((0, 1), (1, -1)):
            slot = 1 + 6 * end if cy > 0 else 2 + 4 * end
            at = BASE + (X - 1) * Y * (1 - end) + (Y - 1) * (cy > 0)
            src = fields.at[which, slot, pl.ds(at, 1), :]
            if way is None:
                yield copy(src, xyrecv.at[which, side, end], device(place, cy, 0), n)
            else:
                target = device(place, 0, 0) if way == 0 else device(None, cy, 0)
                yield copy(src, hop.at[which, side], target, n, 4)

    def x_face(which, place, n):
        end = ends[place]
        at = pl.multiple_of(BASE + (X - 1) * Y * (1 - end), Y)
        yield copy(
            fields.at[which, pl.ds(5 * end, 5), pl.ds(at, Y), :],
            xrecv.at[which, end, :, pl.ds(Y, Y), :], device(place, 0, 0), n,
        )

    def xz_tiles(turn, place, n):
        for side, cz in ((0, 1), (1, -1)):
            yield copy(zsend.at[turn, side], xzrecv.at[turn, side, ends[place]], device(place, 0, cz), n)

    def y_faces(which, n):
        for side, cy in ((0, 1), (1, -1)):
            yield copy(ysend.at[which, side], yrecv.at[which, side], device(None, cy, 0), n)

    def z_faces(turn, n):
        for side, cz in ((0, 1), (1, -1)):
            yield copy(zsend.at[turn, side], zrecv.at[turn, side], device(None, 0, cz), n)
            for k, cy in enumerate((1, -1)):
                row_of = zsend.at[turn, side, pl.ds(Y - 1 if cy > 0 else 0, 1), :]
                yield copy(row_of, yzrecv.at[turn, side, k], device(None, cy, cz), n)

    def wait_all(sem, rows):
        depth = next(d for d in (58, 50, 60, 4, 2) if rows % d == 0)
        some = pops.at[pl.ds(0, rows // depth), pl.ds(0, depth), :]
        pltpu.make_async_copy(some, some, sem).wait()

    def lanes(turn, side, wanted, xs):
        mask = None
        for group in range(10 if turn == 0 else 5):
            if wanted(VELOCITY[ALONG_Z[side][group % 5]]):
                a, b = lane_of(group, xs[0]), lane_of(group, xs[1])
                here = (lane >= a) & (lane <= b)
                mask = here if mask is None else mask | here
        return mask

    def near_tiles(turn):
        tiles = []
        for side in range(2):
            face = zrecv[turn, side]
            up = jnp.where(row == 0, yzrecv[turn, side, 0], pltpu.roll(face, 1, 0))
            down = jnp.where(row == Y - 1, yzrecv[turn, side, 1], pltpu.roll(face, Y - 1, 0))
            tile = jnp.where(lanes(turn, side, lambda c: c[1] > 0, (-1, X)), up, face)
            tiles.append(jnp.where(lanes(turn, side, lambda c: c[1] < 0, (-1, X)), down, tile))
        return tiles

    def streamed(field, x, tiles, member, outer):
        turn = 1 if field == grad else 0
        result = {}
        for v in range(19):
            cx, cy, cz = VELOCITY[v]
            outside = not 0 <= x - cx < X
            if outside != outer:
                continue
            end = 0 if cx > 0 else 1
            if outside:
                value = xrecv[field, end, SLOT[v] - 5 * end, pl.ds(Y - cy, Y), :]
            else:
                value = fields[field, SLOT[v], pl.ds(BASE + Y * (x - cx) - cy, Y), :]
            if cy:
                side = 0 if cy > 0 else 1
                if outside:
                    halo = xyrecv[field, side, end]
                else:
                    halo = yrecv[field, side, ALONG_Y[side].index(v), pl.ds(x - cx, 1), :]
                value = jnp.where(row == (0 if cy > 0 else Y - 1), halo, value)
            if cz:
                side = 0 if cz > 0 else 1
                group = 5 * member + ALONG_Z[side].index(v)
                tile = xzrecv[turn, side, end] if outside else tiles[side]
                at = lane_of(group, (x - cx) % X)
                edge, shift = (0, 1) if cz > 0 else (Z - 1, Z - 1)
                value = jnp.where(
                    lane == edge, pltpu.roll(tile, (edge - at) % Z, 1), pltpu.roll(value, shift, 1)
                )
            result[v] = value
        return result

    def put(field, x, values):
        at = BASE + Y * x
        for v in range(19):
            fields[field, SLOT[v], pl.ds(at, Y), :] = values[v]

    def start(copies):
        for c in copies:
            c.start()

    pltpu.make_async_copy(pops, pops, load_sem.at[0]).wait()

    packed = (nothing, nothing)
    for x in range(X):
        packed = pack_z(lambda v: fields[seed, SLOT[v], pl.ds(BASE + Y * x, Y), :], x, packed, 1)
    pack_y(seed)

    for c in load_rest:
        c.wait()

    for x in range(X):
        f = {v: pops[v, pl.ds(Y * x, Y), :] for v in range(19)}
        collided = collide(f, slip[x], perm[x], kind[x])
        put(col, x, collided)
        packed = pack_z(lambda v: collided[v], x, packed, 0)
    zsend[0, 0], zsend[0, 1] = packed
    pack_y(col)

    both = pl.ds(0, 2)
    pl.semaphore_wait(barrier, 18 - 2 * detours.astype(jnp.int32))
    pl.when(by_x)(lambda: start(xy_rows(both, FARTHER, 0, 0)))
    pl.when(by_y)(lambda: start(xy_rows(both, FARTHER, 0, 1)))
    pl.when(jnp.logical_not(detours))(lambda: start(xy_rows(both, FARTHER, 0)))
    start(z_faces(0, 1))
    start(xz_tiles(0, FARTHER, 0))
    start(y_faces(both, 1))
    start(x_face(both, FARTHER, 0))
    start(xy_rows(both, CLOSER, 0))
    start(xz_tiles(0, CLOSER, 0))
    start(x_face(both, CLOSER, 0))
    middle = [(phase == 1) & (here[1] == gy) for gy in (1, sizes[1] - 1)]
    for side in range(2):
        @pl.when(middle[side])
        def _(side=side):
            wait_all(recv_sem.at[4], 2)
            copy(hop.at[both, side], xyrecv.at[both, side, 0], device(FARTHER, 0, 0), 4, 0).start()

    def inside(x, tiles):
        return streamed(col, x, tiles, 0, False), streamed(seed, x, tiles, 1, False)

    def second(x, tiles, known):
        f = known[0] | streamed(col, x, tiles, 0, True)
        moved = known[1] | streamed(seed, x, tiles, 1, True)
        g = {i: moved[OPPOSITE[i]] for i in range(19)}
        result, of_slip, of_perm = pull(f, g, slip[x], perm[x], kind[x])
        gslip[x], gperm[x] = of_slip, of_perm
        turned = {OPPOSITE[i]: result[i] for i in range(19)}
        put(grad, x, turned)
        return turned

    wait_all(recv_sem.at[1], 180)
    tiles = near_tiles(0)
    packed = (nothing, nothing)
    for x in range(1, X - 1):
        turned = second(x, tiles, inside(x, tiles))
        packed = pack_z(lambda v: turned[v], x, packed, 0)
    known = {x: inside(x, tiles) for x in (0, X - 1)}

    @pl.when(passes_on)
    def _():
        wait_all(recv_sem.at[4], 4)
        start([
            copy(hop.at[both, side], xyrecv.at[both, side, 1], device(None, cy, 0), 4, 0)
            for side, cy in ((0, 1), (1, -1))
        ])

    wait_all(recv_sem.at[0], 200)
    outer = {x: second(x, tiles, known[x]) for x in (0, X - 1)}
    start(xy_rows(grad, FARTHER, 2))
    start(x_face(grad, FARTHER, 2))
    start(xy_rows(grad, CLOSER, 2))
    start(x_face(grad, CLOSER, 2))
    for x, turned in outer.items():
        packed = pack_z(lambda v: turned[v], x, packed, 0)
    zsend[1, 0], zsend[1, 1] = packed
    start(z_faces(1, 3))
    start(xz_tiles(1, FARTHER, 2))
    start(xz_tiles(1, CLOSER, 2))
    pack_y(grad)
    start(y_faces(grad, 3))

    def third(x, tiles, known):
        f = {v: pops[v, pl.ds(Y * x, Y), :] for v in range(19)}
        moved = known | streamed(grad, x, tiles, 0, True)
        g = {i: moved[OPPOSITE[i]] for i in range(19)}
        result, of_slip, of_perm = pull(f, g, slip[x], perm[x], kind[x])
        for v in range(19):
            out[v, x] = result[v]
        gslip[x] = gslip[x] + of_slip
        gperm[x] = gperm[x] + of_perm

    wait_all(recv_sem.at[3], 100)
    tiles = near_tiles(1)
    for x in range(1, X - 1):
        third(x, tiles, streamed(grad, x, tiles, 0, False))
    known = {x: streamed(grad, x, tiles, 0, False) for x in (0, X - 1)}
    for n, rows in ((0, 200), (1, 180), (3, 100)):
        wait_all(send_sem.at[n], rows)

    pl.when(passes_on)(lambda: wait_all(send_sem.at[4], 4))
    pl.when(middle[0] | middle[1])(lambda: wait_all(send_sem.at[4], 2))

    wait_all(recv_sem.at[2], 116)
    for x in (0, X - 1):
        third(x, tiles, known[x])
    wait_all(send_sem.at[2], 116)


def store(out, gslip, gperm, out_hbm, gslip_hbm, gperm_hbm, sem):
    copies = [
        pltpu.make_async_copy(src, dst, sem.at[n])
        for n, (src, dst) in enumerate(((out, out_hbm), (gslip, gslip_hbm), (gperm, gperm_hbm)))
    ]
    for c in copies:
        c.start()
    for c in copies:
        c.wait()


def body(populations, adjoint_seed, wall_slip, permeability, cell_kinds):
    f32 = jnp.float32
    hbm = pl.BlockSpec(memory_space=pltpu.HBM)
    resident = pl.BlockSpec(memory_space=pltpu.VMEM)
    shapes = ((19, X, Y, Z), (X, Y, Z), (X, Y, Z))
    call = pl.pallas_call(
        kernel,
        out_shape=tuple(pltpu.VMEM(shape, f32) for shape in shapes),
        in_specs=[hbm] * 5,
        out_specs=(resident,) * 3,
        scratch_shapes=[
            pltpu.VMEM((19, X * Y, Z), f32),
            pltpu.VMEM((X, Y, Z), f32),
            pltpu.VMEM((X, Y, Z), f32),
            pltpu.VMEM((X, Y, Z), jnp.int32),
            pltpu.VMEM((3, 19, ROWS, Z), f32),
            pltpu.VMEM((3, 2, 5, X, Z), f32),
            pltpu.VMEM((2, 2, Y, Z), f32),
            pltpu.VMEM((3, 2, 5, 3 * Y, Z), f32),
            pltpu.VMEM((3, 2, 5, X, Z), f32),
            pltpu.VMEM((2, 2, Y, Z), f32),
            pltpu.VMEM((2, 2, 1, Z), f32),
            pltpu.VMEM((3, 2, 2, 1, Z), f32),
            pltpu.VMEM((2, 2, 2, Y, Z), f32),
            pltpu.VMEM((2, 2, 2, 1, Z), f32),
            pltpu.SemaphoreType.DMA((5,)),
            pltpu.SemaphoreType.DMA((5,)),
            pltpu.SemaphoreType.DMA((5,)),
        ],
        compiler_params=pltpu.CompilerParams(
            collective_id=0, has_side_effects=True, vmem_limit_bytes=16 * 1024 * 1024
        ),
    )
    operands = (
        populations.reshape(19, X * Y, Z),
        adjoint_seed.reshape(19, X * Y, Z),
        wall_slip,
        permeability,
        cell_kinds,
    )
    results = call(*(pltpu.with_memory_space_constraint(a, pltpu.HBM) for a in operands))
    return pl.pallas_call(
        store,
        out_shape=tuple(jax.ShapeDtypeStruct(shape, f32) for shape in shapes),
        in_specs=[resident] * 3,
        out_specs=(hbm,) * 3,
        scratch_shapes=[pltpu.SemaphoreType.DMA((3,))],
        compiler_params=pltpu.CompilerParams(vmem_limit_bytes=1024 * 1024),
    )(*(pltpu.with_memory_space_constraint(a, pltpu.VMEM) for a in results))


def solution(mesh):
    state, field = P(None, "gx", "gy", "gz"), P("gx", "gy", "gz")
    return jax.shard_map(
        body,
        mesh=mesh,
        in_specs=(state, state, field, field, field),
        out_specs=(state, field, field),
        check_vma=False,
    )
```

```python
import functools

import jax
import jax.numpy as jnp
from jax import lax
from jax.experimental import pallas as pl
from jax.experimental.pallas import tpu as pltpu
from jax.sharding import PartitionSpec as P

MESH = pl.DeviceIdType.MESH
VELOCITY = (
    (0, 0, 0), (1, 0, 0), (-1, 0, 0), (0, 1, 0), (0, -1, 0), (0, 0, 1), (0, 0, -1),
    (1, 1, 0), (-1, -1, 0), (1, -1, 0), (-1, 1, 0), (1, 0, 1), (-1, 0, -1),
    (1, 0, -1), (-1, 0, 1), (0, 1, 1), (0, -1, -1), (0, 1, -1), (0, -1, 1),
)
OPPOSITE = (0, 2, 1, 4, 3, 6, 5, 8, 7, 10, 9, 12, 11, 14, 13, 16, 15, 18, 17)
ORDER = (1, 7, 9, 11, 13, 2, 8, 10, 12, 14, 3, 4, 5, 6, 15, 16, 17, 18, 0)
SLOT = {v: s for s, v in enumerate(ORDER)}
ALONG_Y = ((3, 7, 10, 15, 17), (4, 8, 9, 16, 18))
ALONG_Z = ((5, 11, 14, 15, 18), (6, 12, 13, 16, 17))
W0, W1, W2 = 1.0 / 3.0, 1.0 / 18.0, 1.0 / 36.0
X, Y, Z = 8, 8, 128
BASE = 8
ROWS = 80


def lane_of(group, x):
    return 10 * group + x + 1


def pairs_of(f):
    plus = {i: f[i] + f[i + 1] for i in range(1, 19, 2)}
    minus = {i: f[i] - f[i + 1] for i in range(1, 19, 2)}
    return plus, minus


def vector_of(m):
    return (
        m[1] + ((m[7] + m[9]) + (m[11] + m[13])),
        m[3] + ((m[7] - m[9]) + (m[15] + m[17])),
        m[5] + ((m[11] - m[13]) + (m[15] - m[17])),
    )


def along(i, u):
    total = None
    for c, part in zip(VELOCITY[i], u):
        if c:
            part = part if c > 0 else -part
            total = part if total is None else total + part
    return total


def macroscopic(f, damping):
    plus, minus = pairs_of(f)
    rho = f[0]
    diagonal = (plus[7] + plus[9]) + (plus[11] + plus[13]) + (plus[15] + plus[17])
    rho = rho + ((plus[1] + plus[3]) + (plus[5] + diagonal))
    m = vector_of(minus)
    k = damping / rho
    u = tuple(part * k for part in m)
    usq = u[0] * u[0] + u[1] * u[1] + u[2] * u[2]
    return plus, minus, rho, m, u, usq


def coefficients(slip, perm, kind):
    wall = kind == 2
    keep = jnp.where(wall, slip, 1.0)
    bounce = jnp.where(wall, 1.0 - slip, 0.0)
    damping = jnp.where(kind == 1, perm, 1.0)
    even = 0.5 * bounce - 0.125 * keep
    odd = -0.5 * bounce - 0.125 * keep
    return keep, damping, even, odd


def collide(f, slip, perm, kind):
    keep, damping, even, odd = coefficients(slip, perm, kind)
    plus, minus, rho, m, u, usq = macroscopic(f, damping)
    scale = 1.25 * keep * rho
    base = 1.0 - 1.5 * usq
    out = {0: 2.0 * even * f[0] + W0 * scale * base}
    s1, s2 = W1 * scale, W2 * scale
    s1_base, s2_base = s1 * base, s2 * base
    for i in range(1, 19, 2):
        s, sb = (s1, s1_base) if i < 7 else (s2, s2_base)
        p = along(i, u)
        sp = s * p
        e = sb + 4.5 * (sp * p) + even * plus[i]
        o = 3.0 * sp + odd * minus[i]
        out[i] = e + o
        out[i + 1] = e - o
    return out


def pull(f, g, slip, perm, kind):
    keep, damping, even, odd = coefficients(slip, perm, kind)
    plus, minus, rho, m, u, usq = macroscopic(f, damping)
    gp, gm = pairs_of(g)
    w1g = {i: W1 * gp[i] for i in (1, 3, 5)}
    s_xy, s_xz, s_yz = gp[7] + gp[9], gp[11] + gp[13], gp[15] + gp[17]
    a0 = W0 * g[0] + W1 * (gp[1] + gp[3] + gp[5]) + W2 * (s_xy + s_xz + s_yz)
    b = (
        W1 * gm[1] + W2 * ((gm[7] + gm[9]) + (gm[11] + gm[13])),
        W1 * gm[3] + W2 * ((gm[7] - gm[9]) + (gm[15] + gm[17])),
        W1 * gm[5] + W2 * ((gm[11] - gm[13]) + (gm[15] - gm[17])),
    )
    dxx = w1g[1] + W2 * (s_xy + s_xz)
    dyy = w1g[3] + W2 * (s_xy + s_yz)
    dzz = w1g[5] + W2 * (s_xz + s_yz)
    dxy, dxz, dyz = W2 * (gp[7] - gp[9]), W2 * (gp[11] - gp[13]), W2 * (gp[15] - gp[17])
    du = (
        dxx * u[0] + dxy * u[1] + dxz * u[2],
        dxy * u[0] + dyy * u[1] + dyz * u[2],
        dxz * u[0] + dyz * u[1] + dzz * u[2],
    )
    udu = u[0] * du[0] + u[1] * du[1] + u[2] * du[2]
    ub = u[0] * b[0] + u[1] * b[1] + u[2] * b[2]
    v = tuple(b[i] + 3.0 * du[i] - a0 * u[i] for i in range(3))
    a0usq = a0 * usq
    g_rho = 1.25 * keep * (a0 + 1.5 * a0usq - 4.5 * udu)
    factor = 3.75 * keep * damping
    g_m = tuple(factor * part for part in v)
    out = {0: 2.0 * even * g[0] + g_rho}
    sum_plus, sum_minus = None, None
    for i in range(1, 19, 2):
        s = even * gp[i] + g_rho
        t = odd * gm[i] + along(i, g_m)
        out[i] = s + t
        out[i + 1] = s - t
        a, c = gp[i] * plus[i], gm[i] * minus[i]
        sum_plus = a if sum_plus is None else sum_plus + a
        sum_minus = c if sum_minus is None else sum_minus + c
    of_wall = (
        0.375 * sum_minus
        - 0.625 * sum_plus
        - 1.25 * (g[0] * f[0])
        + 1.25 * rho * (a0 - 1.5 * a0usq + 3.0 * ub + 4.5 * udu)
    )
    of_porous = 3.75 * (v[0] * m[0] + v[1] * m[1] + v[2] * m[2])
    return out, jnp.where(kind == 2, of_wall, 0.0), jnp.where(kind == 1, of_porous, 0.0)


def kernel(
    pop_hbm, seed_hbm, slip_hbm, perm_hbm, kind_hbm,
    out, gslip, gperm,
    pops, slip, perm, kind, fields, ysend, zsend, xrecv, yrecv, zrecv, hop, xyrecv, xzrecv, yzrecv,
    load_sem, send_sem, recv_sem,
):
    here = tuple(lax.axis_index(a) for a in ("gx", "gy", "gz"))
    sizes = tuple(lax.axis_size(a) for a in ("gx", "gy", "gz"))

    above = tuple(lax.rem(h + 1, n) for h, n in zip(here, sizes))
    below = tuple(lax.rem(h + n - 1, n) for h, n in zip(here, sizes))
    col, seed, grad = 0, 1, 2

    odd = lax.rem(here[0], 2)
    ends = (1 - odd, odd)
    across = tuple(jnp.where(end == 0, above[0], below[0]) for end in ends)
    FARTHER, CLOSER = 0, 1

    def device(place, cy, cz):
        gy, gz = ((h, up, down)[c] for c, h, up, down in zip((cy, cz), here[1:], above[1:], below[1:]))
        return (here[0] if place is None else across[place], gy, gz)

    phase, low = lax.rem(here[0], 4), here[1] == 0
    last = here[0] == sizes[0] - 1
    by_x, by_y = low & (here[0] == 0), low & (phase == 1)
    detours = by_x | by_y
    passes_on = low & last

    barrier = pltpu.get_barrier_semaphore()

    def greet(target):
        pl.semaphore_signal(barrier, inc=1, device_id=target, device_id_type=MESH)

    SIDES = ((1, 0), (-1, 0)), ((0, 1), (0, -1))
    for place in (FARTHER, CLOSER):
        for cy, cz in SIDES[0]:
            if place == FARTHER:
                target = device(place, cy, cz)
                spared = (last | (phase == 2)) & (target[1] == 0)
                pl.when(jnp.logical_not(spared))(functools.partial(greet, target))
            else:
                greet(device(place, cy, cz))
        for cy, cz in SIDES[1]:
            greet(device(place, cy, cz))
        greet(device(place, 0, 0))
    for cy in (1, -1, 0):
        for cz in (1, -1, 0):
            if cy or cz:
                greet(device(None, cy, cz))

    load_rest = [
        pltpu.make_async_copy(src, dst, load_sem.at[1 + n])
        for n, (src, dst) in enumerate(
            ((pop_hbm, pops), (slip_hbm, slip), (perm_hbm, perm), (kind_hbm, kind))
        )
    ]
    load_seed = [
        pltpu.make_async_copy(
            seed_hbm.at[i],
            fields.at[seed, SLOT[OPPOSITE[i]], pl.ds(BASE, X * Y), :],
            load_sem.at[0],
        )
        for i in range(19)
    ]
    for c in load_rest + load_seed:
        c.start()

    lane = lax.broadcasted_iota(jnp.int32, (Y, Z), 1)
    row = lax.broadcasted_iota(jnp.int32, (Y, Z), 0)

    def pack_z(values, x, packed, member):
        up, down = packed
        for k, v in enumerate(ALONG_Z[0]):
            at = lane_of(5 * member + k, x)
            up = jnp.where(lane == at, pltpu.roll(values(v), at + 1, 1), up)
        for k, v in enumerate(ALONG_Z[1]):
            at = lane_of(5 * member + k, x)
            down = jnp.where(lane == at, pltpu.roll(values(v), at, 1), down)
        return up, down

    nothing = jnp.zeros((Y, Z), jnp.float32)

    def pack_y(field):
        for side, first in ((0, BASE + Y - 1), (1, BASE)):
            for k, v in enumerate(ALONG_Y[side]):
                ysend[field, side, k] = fields[field, SLOT[v], pl.ds(first, X, stride=Y), :]

    def copy(src, dst, target, n, arrives=None):
        arrives = n if arrives is None else arrives
        return pltpu.make_async_remote_copy(
            src_ref=src, dst_ref=dst, send_sem=send_sem.at[n], recv_sem=recv_sem.at[arrives],
            device_id=target, device_id_type=MESH,
        )

    def xy_rows(which, place, n, way=None):
        end = ends[place]
        for side, cy in ((0, 1), (1, -1)) if way is None else ((1, -1), (0, 1)):
            slot = 1 + 6 * end if cy > 0 else 2 + 4 * end
            at = BASE + (X - 1) * Y * (1 - end) + (Y - 1) * (cy > 0)
            src = fields.at[which, slot, pl.ds(at, 1), :]
            if way is None:
                yield copy(src, xyrecv.at[which, side, end], device(place, cy, 0), n)
            else:
                target = device(place, 0, 0) if way == 0 else device(None, cy, 0)
                yield copy(src, hop.at[which, side], target, n, 4)

    def x_face(which, place, n):
        end = ends[place]
        at = pl.multiple_of(BASE + (X - 1) * Y * (1 - end), Y)
        yield copy(
            fields.at[which, pl.ds(5 * end, 5), pl.ds(at, Y), :],
            xrecv.at[which, end, :, pl.ds(Y, Y), :], device(place, 0, 0), n,
        )

    def xz_tiles(turn, place, n):
        for side, cz in ((0, 1), (1, -1)):
            yield copy(zsend.at[turn, side], xzrecv.at[turn, side, ends[place]], device(place, 0, cz), n)

    def y_faces(which, n):
        for side, cy in ((0, 1), (1, -1)):
            yield copy(ysend.at[which, side], yrecv.at[which, side], device(None, cy, 0), n)

    def z_faces(turn, n):
        for side, cz in ((0, 1), (1, -1)):
            yield copy(zsend.at[turn, side], zrecv.at[turn, side], device(None, 0, cz), n)
            for k, cy in enumerate((1, -1)):
                row_of = zsend.at[turn, side, pl.ds(Y - 1 if cy > 0 else 0, 1), :]
                yield copy(row_of, yzrecv.at[turn, side, k], device(None, cy, cz), n)

    def wait_all(sem, rows):
        depth = next(d for d in (58, 50, 60, 4, 2) if rows % d == 0)
        some = pops.at[pl.ds(0, rows // depth), pl.ds(0, depth), :]
        pltpu.make_async_copy(some, some, sem).wait()

    def lanes(turn, side, wanted, xs):
        mask = None
        for group in range(10 if turn == 0 else 5):
            if wanted(VELOCITY[ALONG_Z[side][group % 5]]):
                a, b = lane_of(group, xs[0]), lane_of(group, xs[1])
                here = (lane >= a) & (lane <= b)
                mask = here if mask is None else mask | here
        return mask

    def near_tiles(turn):
        tiles = []
        for side in range(2):
            face = zrecv[turn, side]
            up = jnp.where(row == 0, yzrecv[turn, side, 0], pltpu.roll(face, 1, 0))
            down = jnp.where(row == Y - 1, yzrecv[turn, side, 1], pltpu.roll(face, Y - 1, 0))
            tile = jnp.where(lanes(turn, side, lambda c: c[1] > 0, (-1, X)), up, face)
            tiles.append(jnp.where(lanes(turn, side, lambda c: c[1] < 0, (-1, X)), down, tile))
        return tiles

    def streamed(field, x, tiles, member, outer):
        turn = 1 if field == grad else 0
        result = {}
        for v in range(19):
            cx, cy, cz = VELOCITY[v]
            outside = not 0 <= x - cx < X
            if outside != outer:
                continue
            end = 0 if cx > 0 else 1
            if outside:
                value = xrecv[field, end, SLOT[v] - 5 * end, pl.ds(Y - cy, Y), :]
            else:
                value = fields[field, SLOT[v], pl.ds(BASE + Y * (x - cx) - cy, Y), :]
            if cy:
                side = 0 if cy > 0 else 1
                if outside:
                    halo = xyrecv[field, side, end]
                else:
                    halo = yrecv[field, side, ALONG_Y[side].index(v), pl.ds(x - cx, 1), :]
                value = jnp.where(row == (0 if cy > 0 else Y - 1), halo, value)
            if cz:
                side = 0 if cz > 0 else 1
                group = 5 * member + ALONG_Z[side].index(v)
                tile = xzrecv[turn, side, end] if outside else tiles[side]
                at = lane_of(group, (x - cx) % X)
                edge, shift = (0, 1) if cz > 0 else (Z - 1, Z - 1)
                value = jnp.where(
                    lane == edge, pltpu.roll(tile, (edge - at) % Z, 1), pltpu.roll(value, shift, 1)
                )
            result[v] = value
        return result

    def put(field, x, values):
        at = BASE + Y * x
        for v in range(19):
            fields[field, SLOT[v], pl.ds(at, Y), :] = values[v]

    def start(copies):
        for c in copies:
            c.start()

    pltpu.make_async_copy(pops, pops, load_sem.at[0]).wait()

    packed = (nothing, nothing)
    for x in range(X):
        packed = pack_z(lambda v: fields[seed, SLOT[v], pl.ds(BASE + Y * x, Y), :], x, packed, 1)
    pack_y(seed)

    for c in load_rest:
        c.wait()

    for x in range(X):
        f = {v: pops[v, pl.ds(Y * x, Y), :] for v in range(19)}
        collided = collide(f, slip[x], perm[x], kind[x])
        put(col, x, collided)
        packed = pack_z(lambda v: collided[v], x, packed, 0)
    zsend[0, 0], zsend[0, 1] = packed
    pack_y(col)

    both = pl.ds(0, 2)
    pl.semaphore_wait(barrier, 18 - 2 * detours.astype(jnp.int32))
    pl.when(by_x)(lambda: start(xy_rows(both, FARTHER, 0, 0)))
    pl.when(by_y)(lambda: start(xy_rows(both, FARTHER, 0, 1)))
    pl.when(jnp.logical_not(detours))(lambda: start(xy_rows(both, FARTHER, 0)))
    start(z_faces(0, 1))
    start(xz_tiles(0, FARTHER, 0))
    start(y_faces(both, 1))
    start(x_face(both, FARTHER, 0))
    start(xy_rows(both, CLOSER, 0))
    start(xz_tiles(0, CLOSER, 0))
    start(x_face(both, CLOSER, 0))
    middle = [(phase == 1) & (here[1] == gy) for gy in (1, sizes[1] - 1)]
    for side in range(2):
        @pl.when(middle[side])
        def _(side=side):
            wait_all(recv_sem.at[4], 2)
            copy(hop.at[both, side], xyrecv.at[both, side, 0], device(FARTHER, 0, 0), 4, 0).start()

    def inside(x, tiles):
        return streamed(col, x, tiles, 0, False), streamed(seed, x, tiles, 1, False)

    def second(x, tiles, known):
        f = known[0] | streamed(col, x, tiles, 0, True)
        moved = known[1] | streamed(seed, x, tiles, 1, True)
        g = {i: moved[OPPOSITE[i]] for i in range(19)}
        result, of_slip, of_perm = pull(f, g, slip[x], perm[x], kind[x])
        gslip[x], gperm[x] = of_slip, of_perm
        turned = {OPPOSITE[i]: result[i] for i in range(19)}
        put(grad, x, turned)
        return turned

    wait_all(recv_sem.at[1], 180)
    tiles = near_tiles(0)
    packed = (nothing, nothing)
    for x in range(1, X - 1):
        turned = second(x, tiles, inside(x, tiles))
        packed = pack_z(lambda v: turned[v], x, packed, 0)
    known = {x: inside(x, tiles) for x in (0, X - 1)}

    @pl.when(passes_on)
    def _():
        wait_all(recv_sem.at[4], 4)
        start([
            copy(hop.at[both, side], xyrecv.at[both, side, 1], device(None, cy, 0), 4, 0)
            for side, cy in ((1, -1), (0, 1))
        ])

    wait_all(recv_sem.at[0], 200)
    outer = {x: second(x, tiles, known[x]) for x in (0, X - 1)}
    start(xy_rows(grad, FARTHER, 2))
    start(x_face(grad, FARTHER, 2))
    start(xy_rows(grad, CLOSER, 2))
    start(x_face(grad, CLOSER, 2))
    for x, turned in outer.items():
        packed = pack_z(lambda v: turned[v], x, packed, 0)
    zsend[1, 0], zsend[1, 1] = packed
    start(z_faces(1, 3))
    start(xz_tiles(1, FARTHER, 2))
    start(xz_tiles(1, CLOSER, 2))
    pack_y(grad)
    start(y_faces(grad, 3))

    def third(x, tiles, known):
        f = {v: pops[v, pl.ds(Y * x, Y), :] for v in range(19)}
        moved = known | streamed(grad, x, tiles, 0, True)
        g = {i: moved[OPPOSITE[i]] for i in range(19)}
        result, of_slip, of_perm = pull(f, g, slip[x], perm[x], kind[x])
        for v in range(19):
            out[v, x] = result[v]
        gslip[x] = gslip[x] + of_slip
        gperm[x] = gperm[x] + of_perm

    wait_all(recv_sem.at[3], 100)
    tiles = near_tiles(1)
    for x in range(1, X - 1):
        third(x, tiles, streamed(grad, x, tiles, 0, False))
    known = {x: streamed(grad, x, tiles, 0, False) for x in (0, X - 1)}
    for n, rows in ((0, 200), (1, 180), (3, 100)):
        wait_all(send_sem.at[n], rows)

    pl.when(passes_on)(lambda: wait_all(send_sem.at[4], 4))
    pl.when(middle[0] | middle[1])(lambda: wait_all(send_sem.at[4], 2))

    wait_all(recv_sem.at[2], 116)
    for x in (0, X - 1):
        third(x, tiles, known[x])
    wait_all(send_sem.at[2], 116)


def store(out, gslip, gperm, out_hbm, gslip_hbm, gperm_hbm, sem):
    copies = [
        pltpu.make_async_copy(src, dst, sem.at[n])
        for n, (src, dst) in enumerate(((out, out_hbm), (gslip, gslip_hbm), (gperm, gperm_hbm)))
    ]
    for c in copies:
        c.start()
    for c in copies:
        c.wait()


def body(populations, adjoint_seed, wall_slip, permeability, cell_kinds):
    f32 = jnp.float32
    hbm = pl.BlockSpec(memory_space=pltpu.HBM)
    resident = pl.BlockSpec(memory_space=pltpu.VMEM)
    shapes = ((19, X, Y, Z), (X, Y, Z), (X, Y, Z))
    call = pl.pallas_call(
        kernel,
        out_shape=tuple(pltpu.VMEM(shape, f32) for shape in shapes),
        in_specs=[hbm] * 5,
        out_specs=(resident,) * 3,
        scratch_shapes=[
            pltpu.VMEM((19, X * Y, Z), f32),
            pltpu.VMEM((X, Y, Z), f32),
            pltpu.VMEM((X, Y, Z), f32),
            pltpu.VMEM((X, Y, Z), jnp.int32),
            pltpu.VMEM((3, 19, ROWS, Z), f32),
            pltpu.VMEM((3, 2, 5, X, Z), f32),
            pltpu.VMEM((2, 2, Y, Z), f32),
            pltpu.VMEM((3, 2, 5, 3 * Y, Z), f32),
            pltpu.VMEM((3, 2, 5, X, Z), f32),
            pltpu.VMEM((2, 2, Y, Z), f32),
            pltpu.VMEM((2, 2, 1, Z), f32),
            pltpu.VMEM((3, 2, 2, 1, Z), f32),
            pltpu.VMEM((2, 2, 2, Y, Z), f32),
            pltpu.VMEM((2, 2, 2, 1, Z), f32),
            pltpu.SemaphoreType.DMA((5,)),
            pltpu.SemaphoreType.DMA((5,)),
            pltpu.SemaphoreType.DMA((5,)),
        ],
        compiler_params=pltpu.CompilerParams(
            collective_id=0, has_side_effects=True, vmem_limit_bytes=16 * 1024 * 1024
        ),
    )
    operands = (
        populations.reshape(19, X * Y, Z),
        adjoint_seed.reshape(19, X * Y, Z),
        wall_slip,
        permeability,
        cell_kinds,
    )
    results = call(*(pltpu.with_memory_space_constraint(a, pltpu.HBM) for a in operands))
    return pl.pallas_call(
        store,
        out_shape=tuple(jax.ShapeDtypeStruct(shape, f32) for shape in shapes),
        in_specs=[resident] * 3,
        out_specs=(hbm,) * 3,
        scratch_shapes=[pltpu.SemaphoreType.DMA((3,))],
        compiler_params=pltpu.CompilerParams(vmem_limit_bytes=1024 * 1024),
    )(*(pltpu.with_memory_space_constraint(a, pltpu.VMEM) for a in results))


def solution(mesh):
    state, field = P(None, "gx", "gy", "gz"), P("gx", "gy", "gz")
    return jax.shard_map(
        body,
        mesh=mesh,
        in_specs=(state, state, field, field, field),
        out_specs=(state, field, field),
        check_vma=False,
    )
```

```python
import functools

import jax
import jax.numpy as jnp
from jax import lax
from jax.experimental import pallas as pl
from jax.experimental.pallas import tpu as pltpu
from jax.sharding import PartitionSpec as P

MESH = pl.DeviceIdType.MESH
VELOCITY = (
    (0, 0, 0), (1, 0, 0), (-1, 0, 0), (0, 1, 0), (0, -1, 0), (0, 0, 1), (0, 0, -1),
    (1, 1, 0), (-1, -1, 0), (1, -1, 0), (-1, 1, 0), (1, 0, 1), (-1, 0, -1),
    (1, 0, -1), (-1, 0, 1), (0, 1, 1), (0, -1, -1), (0, 1, -1), (0, -1, 1),
)
OPPOSITE = (0, 2, 1, 4, 3, 6, 5, 8, 7, 10, 9, 12, 11, 14, 13, 16, 15, 18, 17)
ORDER = (1, 7, 9, 11, 13, 2, 8, 10, 12, 14, 3, 4, 5, 6, 15, 16, 17, 18, 0)
SLOT = {v: s for s, v in enumerate(ORDER)}
ALONG_Y = ((3, 7, 10, 15, 17), (4, 8, 9, 16, 18))
ALONG_Z = ((5, 11, 14, 15, 18), (6, 12, 13, 16, 17))
W0, W1, W2 = 1.0 / 3.0, 1.0 / 18.0, 1.0 / 36.0
X, Y, Z = 8, 8, 128
BASE = 8
ROWS = 80


def lane_of(group, x):
    return 10 * group + x + 1


def pairs_of(f):
    plus = {i: f[i] + f[i + 1] for i in range(1, 19, 2)}
    minus = {i: f[i] - f[i + 1] for i in range(1, 19, 2)}
    return plus, minus


def vector_of(m):
    return (
        m[1] + ((m[7] + m[9]) + (m[11] + m[13])),
        m[3] + ((m[7] - m[9]) + (m[15] + m[17])),
        m[5] + ((m[11] - m[13]) + (m[15] - m[17])),
    )


def along(i, u):
    total = None
    for c, part in zip(VELOCITY[i], u):
        if c:
            part = part if c > 0 else -part
            total = part if total is None else total + part
    return total


def macroscopic(f, damping):
    plus, minus = pairs_of(f)
    rho = f[0]
    diagonal = (plus[7] + plus[9]) + (plus[11] + plus[13]) + (plus[15] + plus[17])
    rho = rho + ((plus[1] + plus[3]) + (plus[5] + diagonal))
    m = vector_of(minus)
    k = damping / rho
    u = tuple(part * k for part in m)
    usq = u[0] * u[0] + u[1] * u[1] + u[2] * u[2]
    return plus, minus, rho, m, u, usq


def coefficients(slip, perm, kind):
    wall = kind == 2
    keep = jnp.where(wall, slip, 1.0)
    bounce = jnp.where(wall, 1.0 - slip, 0.0)
    damping = jnp.where(kind == 1, perm, 1.0)
    even = 0.5 * bounce - 0.125 * keep
    odd = -0.5 * bounce - 0.125 * keep
    return keep, damping, even, odd


def collide(f, slip, perm, kind):
    keep, damping, even, odd = coefficients(slip, perm, kind)
    plus, minus, rho, m, u, usq = macroscopic(f, damping)
    scale = 1.25 * keep * rho
    base = 1.0 - 1.5 * usq
    out = {0: 2.0 * even * f[0] + W0 * scale * base}
    s1, s2 = W1 * scale, W2 * scale
    s1_base, s2_base = s1 * base, s2 * base
    for i in range(1, 19, 2):
        s, sb = (s1, s1_base) if i < 7 else (s2, s2_base)
        p = along(i, u)
        sp = s * p
        e = sb + 4.5 * (sp * p) + even * plus[i]
        o = 3.0 * sp + odd * minus[i]
        out[i] = e + o
        out[i + 1] = e - o
    return out


def pull(f, g, slip, perm, kind):
    keep, damping, even, odd = coefficients(slip, perm, kind)
    plus, minus, rho, m, u, usq = macroscopic(f, damping)
    gp, gm = pairs_of(g)
    w1g = {i: W1 * gp[i] for i in (1, 3, 5)}
    s_xy, s_xz, s_yz = gp[7] + gp[9], gp[11] + gp[13], gp[15] + gp[17]
    a0 = W0 * g[0] + W1 * (gp[1] + gp[3] + gp[5]) + W2 * (s_xy + s_xz + s_yz)
    b = (
        W1 * gm[1] + W2 * ((gm[7] + gm[9]) + (gm[11] + gm[13])),
        W1 * gm[3] + W2 * ((gm[7] - gm[9]) + (gm[15] + gm[17])),
        W1 * gm[5] + W2 * ((gm[11] - gm[13]) + (gm[15] - gm[17])),
    )
    dxx = w1g[1] + W2 * (s_xy + s_xz)
    dyy = w1g[3] + W2 * (s_xy + s_yz)
    dzz = w1g[5] + W2 * (s_xz + s_yz)
    dxy, dxz, dyz = W2 * (gp[7] - gp[9]), W2 * (gp[11] - gp[13]), W2 * (gp[15] - gp[17])
    du = (
        dxx * u[0] + dxy * u[1] + dxz * u[2],
        dxy * u[0] + dyy * u[1] + dyz * u[2],
        dxz * u[0] + dyz * u[1] + dzz * u[2],
    )
    udu = u[0] * du[0] + u[1] * du[1] + u[2] * du[2]
    ub = u[0] * b[0] + u[1] * b[1] + u[2] * b[2]
    v = tuple(b[i] + 3.0 * du[i] - a0 * u[i] for i in range(3))
    a0usq = a0 * usq
    g_rho = 1.25 * keep * (a0 + 1.5 * a0usq - 4.5 * udu)
    factor = 3.75 * keep * damping
    g_m = tuple(factor * part for part in v)
    out = {0: 2.0 * even * g[0] + g_rho}
    sum_plus, sum_minus = None, None
    for i in range(1, 19, 2):
        s = even * gp[i] + g_rho
        t = odd * gm[i] + along(i, g_m)
        out[i] = s + t
        out[i + 1] = s - t
        a, c = gp[i] * plus[i], gm[i] * minus[i]
        sum_plus = a if sum_plus is None else sum_plus + a
        sum_minus = c if sum_minus is None else sum_minus + c
    of_wall = (
        0.375 * sum_minus
        - 0.625 * sum_plus
        - 1.25 * (g[0] * f[0])
        + 1.25 * rho * (a0 - 1.5 * a0usq + 3.0 * ub + 4.5 * udu)
    )
    of_porous = 3.75 * (v[0] * m[0] + v[1] * m[1] + v[2] * m[2])
    return out, jnp.where(kind == 2, of_wall, 0.0), jnp.where(kind == 1, of_porous, 0.0)


def kernel(
    pop_hbm, seed_hbm, slip_hbm, perm_hbm, kind_hbm,
    out, gslip, gperm,
    pops, slip, perm, kind, fields, ysend, zsend, xrecv, yrecv, zrecv, hop, xyrecv, xzrecv, yzrecv,
    load_sem, send_sem, recv_sem,
):
    here = tuple(lax.axis_index(a) for a in ("gx", "gy", "gz"))
    sizes = tuple(lax.axis_size(a) for a in ("gx", "gy", "gz"))

    above = tuple(lax.rem(h + 1, n) for h, n in zip(here, sizes))
    below = tuple(lax.rem(h + n - 1, n) for h, n in zip(here, sizes))
    col, seed, grad = 0, 1, 2

    odd = lax.rem(here[0], 2)
    ends = (1 - odd, odd)
    across = tuple(jnp.where(end == 0, above[0], below[0]) for end in ends)
    FARTHER, CLOSER = 0, 1

    def device(place, cy, cz):
        gy, gz = ((h, up, down)[c] for c, h, up, down in zip((cy, cz), here[1:], above[1:], below[1:]))
        return (here[0] if place is None else across[place], gy, gz)

    phase, low = lax.rem(here[0], 4), here[1] == 0
    last = here[0] == sizes[0] - 1
    by_x, by_y = low & (here[0] == 0), low & (phase == 1)
    detours = by_x | by_y
    passes_on = low & last

    barrier = pltpu.get_barrier_semaphore()

    def greet(target):
        pl.semaphore_signal(barrier, inc=1, device_id=target, device_id_type=MESH)

    SIDES = ((1, 0), (-1, 0)), ((0, 1), (0, -1))
    for place in (FARTHER, CLOSER):
        for cy, cz in SIDES[0]:
            if place == FARTHER:
                target = device(place, cy, cz)
                spared = (last | (phase == 2)) & (target[1] == 0)
                pl.when(jnp.logical_not(spared))(functools.partial(greet, target))
            else:
                greet(device(place, cy, cz))
        greet(device(place, 0, 0))
        for cy, cz in SIDES[1]:
            greet(device(place, cy, cz))
    for cy in (1, -1, 0):
        for cz in (1, -1, 0):
            if cy or cz:
                greet(device(None, cy, cz))

    load_rest = [
        pltpu.make_async_copy(src, dst, load_sem.at[1 + n])
        for n, (src, dst) in enumerate(
            ((pop_hbm, pops), (slip_hbm, slip), (perm_hbm, perm), (kind_hbm, kind))
        )
    ]
    load_seed = [
        pltpu.make_async_copy(
            seed_hbm.at[i],
            fields.at[seed, SLOT[OPPOSITE[i]], pl.ds(BASE, X * Y), :],
            load_sem.at[0],
        )
        for i in range(19)
    ]
    for c in load_rest + load_seed:
        c.start()

    lane = lax.broadcasted_iota(jnp.int32, (Y, Z), 1)
    row = lax.broadcasted_iota(jnp.int32, (Y, Z), 0)

    def pack_z(values, x, packed, member):
        up, down = packed
        for k, v in enumerate(ALONG_Z[0]):
            at = lane_of(5 * member + k, x)
            up = jnp.where(lane == at, pltpu.roll(values(v), at + 1, 1), up)
        for k, v in enumerate(ALONG_Z[1]):
            at = lane_of(5 * member + k, x)
            down = jnp.where(lane == at, pltpu.roll(values(v), at, 1), down)
        return up, down

    nothing = jnp.zeros((Y, Z), jnp.float32)

    def pack_y(field):
        for side, first in ((0, BASE + Y - 1), (1, BASE)):
            for k, v in enumerate(ALONG_Y[side]):
                ysend[field, side, k] = fields[field, SLOT[v], pl.ds(first, X, stride=Y), :]

    def copy(src, dst, target, n, arrives=None):
        arrives = n if arrives is None else arrives
        return pltpu.make_async_remote_copy(
            src_ref=src, dst_ref=dst, send_sem=send_sem.at[n], recv_sem=recv_sem.at[arrives],
            device_id=target, device_id_type=MESH,
        )

    def xy_rows(which, place, n, way=None):
        end = ends[place]
        for side, cy in ((0, 1), (1, -1)):
            slot = 1 + 6 * end if cy > 0 else 2 + 4 * end
            at = BASE + (X - 1) * Y * (1 - end) + (Y - 1) * (cy > 0)
            src = fields.at[which, slot, pl.ds(at, 1), :]
            if way is None:
                yield copy(src, xyrecv.at[which, side, end], device(place, cy, 0), n)
            else:
                target = device(place, 0, 0) if way == 0 else device(None, cy, 0)
                yield copy(src, hop.at[which, side], target, n, 4)

    def x_face(which, place, n):
        end = ends[place]
        at = pl.multiple_of(BASE + (X - 1) * Y * (1 - end), Y)
        yield copy(
            fields.at[which, pl.ds(5 * end, 5), pl.ds(at, Y), :],
            xrecv.at[which, end, :, pl.ds(Y, Y), :], device(place, 0, 0), n,
        )

    def xz_tiles(turn, place, n):
        for side, cz in ((0, 1), (1, -1)):
            yield copy(zsend.at[turn, side], xzrecv.at[turn, side, ends[place]], device(place, 0, cz), n)

    def y_faces(which, n):
        for side, cy in ((0, 1), (1, -1)):
            yield copy(ysend.at[which, side], yrecv.at[which, side], device(None, cy, 0), n)

    def z_faces(turn, n):
        for side, cz in ((0, 1), (1, -1)):
            yield copy(zsend.at[turn, side], zrecv.at[turn, side], device(None, 0, cz), n)
            for k, cy in enumerate((1, -1)):
                row_of = zsend.at[turn, side, pl.ds(Y - 1 if cy > 0 else 0, 1), :]
                yield copy(row_of, yzrecv.at[turn, side, k], device(None, cy, cz), n)

    def wait_all(sem, rows):
        depth = next(d for d in (58, 50, 60, 4, 2) if rows % d == 0)
        some = pops.at[pl.ds(0, rows // depth), pl.ds(0, depth), :]
        pltpu.make_async_copy(some, some, sem).wait()

    def lanes(turn, side, wanted, xs):
        mask = None
        for group in range(10 if turn == 0 else 5):
            if wanted(VELOCITY[ALONG_Z[side][group % 5]]):
                a, b = lane_of(group, xs[0]), lane_of(group, xs[1])
                here = (lane >= a) & (lane <= b)
                mask = here if mask is None else mask | here
        return mask

    def near_tiles(turn):
        tiles = []
        for side in range(2):
            face = zrecv[turn, side]
            up = jnp.where(row == 0, yzrecv[turn, side, 0], pltpu.roll(face, 1, 0))
            down = jnp.where(row == Y - 1, yzrecv[turn, side, 1], pltpu.roll(face, Y - 1, 0))
            tile = jnp.where(lanes(turn, side, lambda c: c[1] > 0, (-1, X)), up, face)
            tiles.append(jnp.where(lanes(turn, side, lambda c: c[1] < 0, (-1, X)), down, tile))
        return tiles

    def streamed(field, x, tiles, member, outer):
        turn = 1 if field == grad else 0
        result = {}
        for v in range(19):
            cx, cy, cz = VELOCITY[v]
            outside = not 0 <= x - cx < X
            if outside != outer:
                continue
            end = 0 if cx > 0 else 1
            if outside:
                value = xrecv[field, end, SLOT[v] - 5 * end, pl.ds(Y - cy, Y), :]
            else:
                value = fields[field, SLOT[v], pl.ds(BASE + Y * (x - cx) - cy, Y), :]
            if cy:
                side = 0 if cy > 0 else 1
                if outside:
                    halo = xyrecv[field, side, end]
                else:
                    halo = yrecv[field, side, ALONG_Y[side].index(v), pl.ds(x - cx, 1), :]
                value = jnp.where(row == (0 if cy > 0 else Y - 1), halo, value)
            if cz:
                side = 0 if cz > 0 else 1
                group = 5 * member + ALONG_Z[side].index(v)
                tile = xzrecv[turn, side, end] if outside else tiles[side]
                at = lane_of(group, (x - cx) % X)
                edge, shift = (0, 1) if cz > 0 else (Z - 1, Z - 1)
                value = jnp.where(
                    lane == edge, pltpu.roll(tile, (edge - at) % Z, 1), pltpu.roll(value, shift, 1)
                )
            result[v] = value
        return result

    def put(field, x, values):
        at = BASE + Y * x
        for v in range(19):
            fields[field, SLOT[v], pl.ds(at, Y), :] = values[v]

    def start(copies):
        for c in copies:
            c.start()

    pltpu.make_async_copy(pops, pops, load_sem.at[0]).wait()

    packed = (nothing, nothing)
    for x in range(X):
        packed = pack_z(lambda v: fields[seed, SLOT[v], pl.ds(BASE + Y * x, Y), :], x, packed, 1)
    pack_y(seed)

    for c in load_rest:
        c.wait()

    for x in range(X):
        f = {v: pops[v, pl.ds(Y * x, Y), :] for v in range(19)}
        collided = collide(f, slip[x], perm[x], kind[x])
        put(col, x, collided)
        packed = pack_z(lambda v: collided[v], x, packed, 0)
    zsend[0, 0], zsend[0, 1] = packed
    pack_y(col)

    both = pl.ds(0, 2)
    pl.semaphore_wait(barrier, 18 - 2 * detours.astype(jnp.int32))
    pl.when(by_x)(lambda: start(xy_rows(both, FARTHER, 0, 0)))
    pl.when(by_y)(lambda: start(xy_rows(both, FARTHER, 0, 1)))
    pl.when(jnp.logical_not(detours))(lambda: start(xy_rows(both, FARTHER, 0)))
    start(z_faces(0, 1))
    start(xz_tiles(0, FARTHER, 0))
    start(y_faces(both, 1))
    start(x_face(both, FARTHER, 0))
    start(xy_rows(both, CLOSER, 0))
    start(xz_tiles(0, CLOSER, 0))
    start(x_face(both, CLOSER, 0))
    middle = [(phase == 1) & (here[1] == gy) for gy in (1, sizes[1] - 1)]
    for side in range(2):
        @pl.when(middle[side])
        def _(side=side):
            wait_all(recv_sem.at[4], 2)
            copy(hop.at[both, side], xyrecv.at[both, side, 0], device(FARTHER, 0, 0), 4, 0).start()

    def inside(x, tiles):
        return streamed(col, x, tiles, 0, False), streamed(seed, x, tiles, 1, False)

    def second(x, tiles, known):
        f = known[0] | streamed(col, x, tiles, 0, True)
        moved = known[1] | streamed(seed, x, tiles, 1, True)
        g = {i: moved[OPPOSITE[i]] for i in range(19)}
        result, of_slip, of_perm = pull(f, g, slip[x], perm[x], kind[x])
        gslip[x], gperm[x] = of_slip, of_perm
        turned = {OPPOSITE[i]: result[i] for i in range(19)}
        put(grad, x, turned)
        return turned

    wait_all(recv_sem.at[1], 180)
    tiles = near_tiles(0)
    packed = (nothing, nothing)
    for x in range(1, X - 1):
        turned = second(x, tiles, inside(x, tiles))
        packed = pack_z(lambda v: turned[v], x, packed, 0)
    known = {x: inside(x, tiles) for x in (0, X - 1)}

    @pl.when(passes_on)
    def _():
        wait_all(recv_sem.at[4], 4)
        start([
            copy(hop.at[both, side], xyrecv.at[both, side, 1], device(None, cy, 0), 4, 0)
            for side, cy in ((0, 1), (1, -1))
        ])

    wait_all(recv_sem.at[0], 200)
    outer = {x: second(x, tiles, known[x]) for x in (0, X - 1)}
    start(xy_rows(grad, FARTHER, 2))
    start(x_face(grad, FARTHER, 2))
    start(xy_rows(grad, CLOSER, 2))
    start(x_face(grad, CLOSER, 2))
    for x, turned in outer.items():
        packed = pack_z(lambda v: turned[v], x, packed, 0)
    zsend[1, 0], zsend[1, 1] = packed
    start(z_faces(1, 3))
    start(xz_tiles(1, FARTHER, 2))
    start(xz_tiles(1, CLOSER, 2))
    pack_y(grad)
    start(y_faces(grad, 3))

    def third(x, tiles, known):
        f = {v: pops[v, pl.ds(Y * x, Y), :] for v in range(19)}
        moved = known | streamed(grad, x, tiles, 0, True)
        g = {i: moved[OPPOSITE[i]] for i in range(19)}
        result, of_slip, of_perm = pull(f, g, slip[x], perm[x], kind[x])
        for v in range(19):
            out[v, x] = result[v]
        gslip[x] = gslip[x] + of_slip
        gperm[x] = gperm[x] + of_perm

    wait_all(recv_sem.at[3], 100)
    tiles = near_tiles(1)
    for x in range(1, X - 1):
        third(x, tiles, streamed(grad, x, tiles, 0, False))
    known = {x: streamed(grad, x, tiles, 0, False) for x in (0, X - 1)}
    for n, rows in ((0, 200), (1, 180), (3, 100)):
        wait_all(send_sem.at[n], rows)

    pl.when(passes_on)(lambda: wait_all(send_sem.at[4], 4))
    pl.when(middle[0] | middle[1])(lambda: wait_all(send_sem.at[4], 2))

    wait_all(recv_sem.at[2], 116)
    for x in (0, X - 1):
        third(x, tiles, known[x])
    wait_all(send_sem.at[2], 116)


def store(out, gslip, gperm, out_hbm, gslip_hbm, gperm_hbm, sem):
    copies = [
        pltpu.make_async_copy(src, dst, sem.at[n])
        for n, (src, dst) in enumerate(((out, out_hbm), (gslip, gslip_hbm), (gperm, gperm_hbm)))
    ]
    for c in copies:
        c.start()
    for c in copies:
        c.wait()


def body(populations, adjoint_seed, wall_slip, permeability, cell_kinds):
    f32 = jnp.float32
    hbm = pl.BlockSpec(memory_space=pltpu.HBM)
    resident = pl.BlockSpec(memory_space=pltpu.VMEM)
    shapes = ((19, X, Y, Z), (X, Y, Z), (X, Y, Z))
    call = pl.pallas_call(
        kernel,
        out_shape=tuple(pltpu.VMEM(shape, f32) for shape in shapes),
        in_specs=[hbm] * 5,
        out_specs=(resident,) * 3,
        scratch_shapes=[
            pltpu.VMEM((19, X * Y, Z), f32),
            pltpu.VMEM((X, Y, Z), f32),
            pltpu.VMEM((X, Y, Z), f32),
            pltpu.VMEM((X, Y, Z), jnp.int32),
            pltpu.VMEM((3, 19, ROWS, Z), f32),
            pltpu.VMEM((3, 2, 5, X, Z), f32),
            pltpu.VMEM((2, 2, Y, Z), f32),
            pltpu.VMEM((3, 2, 5, 3 * Y, Z), f32),
            pltpu.VMEM((3, 2, 5, X, Z), f32),
            pltpu.VMEM((2, 2, Y, Z), f32),
            pltpu.VMEM((2, 2, 1, Z), f32),
            pltpu.VMEM((3, 2, 2, 1, Z), f32),
            pltpu.VMEM((2, 2, 2, Y, Z), f32),
            pltpu.VMEM((2, 2, 2, 1, Z), f32),
            pltpu.SemaphoreType.DMA((5,)),
            pltpu.SemaphoreType.DMA((5,)),
            pltpu.SemaphoreType.DMA((5,)),
        ],
        compiler_params=pltpu.CompilerParams(
            collective_id=0, has_side_effects=True, vmem_limit_bytes=16 * 1024 * 1024
        ),
    )
    operands = (
        populations.reshape(19, X * Y, Z),
        adjoint_seed.reshape(19, X * Y, Z),
        wall_slip,
        permeability,
        cell_kinds,
    )
    results = call(*(pltpu.with_memory_space_constraint(a, pltpu.HBM) for a in operands))
    return pl.pallas_call(
        store,
        out_shape=tuple(jax.ShapeDtypeStruct(shape, f32) for shape in shapes),
        in_specs=[resident] * 3,
        out_specs=(hbm,) * 3,
        scratch_shapes=[pltpu.SemaphoreType.DMA((3,))],
        compiler_params=pltpu.CompilerParams(vmem_limit_bytes=1024 * 1024),
    )(*(pltpu.with_memory_space_constraint(a, pltpu.VMEM) for a in results))


def solution(mesh):
    state, field = P(None, "gx", "gy", "gz"), P("gx", "gy", "gz")
    return jax.shard_map(
        body,
        mesh=mesh,
        in_specs=(state, state, field, field, field),
        out_specs=(state, field, field),
        check_vma=False,
    )
```
